512 devices in a mesh: seq: 64 (over y, x, core), head: 8 (over z).
Axes of the slice: x: 4, y: 8, z: 8, core: 2. Of those that a mesh axis runs over, the one named last changes fastest.
Arguments:
- x_proj: bfloat16 [8192, 8192], P(('seq', 'head')), may hold values from -6 to 6
- z_gate: bfloat16 [8192, 8192], P(('seq', 'head')), may hold values from -6 to 6
- out_grad: bfloat16 [8192, 8192], P(('seq', 'head')), may hold values from -6 to 6
- b_proj: bfloat16 [8192, 1024], P(('seq', 'head')), may hold values from -1 to 1
- c_proj: bfloat16 [8192, 1024], P(('seq', 'head')), may hold values from -1 to 1
- dt_raw: bfloat16 [8192, 128], P(('seq', 'head')), may hold values from -3 to 3
- dt_bias: float32 [128], P('head'), may hold values from -0.5 to 0.5
- a_log: float32 [128], P('head')
- d_skip: float32 [128], P('head'), may hold values from 0.5 to 1.5
Outputs:
- grad_x: bfloat16 [8192, 8192], P(('seq', 'head'))
- grad_z: bfloat16 [8192, 8192], P(('seq', 'head'))
- grad_b: bfloat16 [8192, 1024], P(('seq', 'head'))
- grad_c: bfloat16 [8192, 1024], P(('seq', 'head'))
- grad_dt: bfloat16 [8192, 128], P(('seq', 'head'))
- grad_bias: float32 [128], P('head')
- grad_alog: float32 [128], P('head')
- grad_dskip: float32 [128], P('head')
The draws below stay inside these ranges and needn't reach their ends.
All inputs are finite; a program needn't handle non-finite values.
Results may differ from the reference program's by a relative error of at most 0.0103.
Values may be sent and summed in bfloat16 or wider, within the bound.
A program may use at most 192 MiB of HBM per device.

```python
import jax
import jax.numpy as jnp
from jax import lax

HEADS = 128
HEAD_DIM = 64
STATE = 128
GROUPS = 8
SEQ_DEV = 128
TOKENS = 8192
INNER = 8192
PROJ_BC = 1024


def draw_a_log(key, part):
    key = jax.random.fold_in(key, 7)
    pick_key, slow_key, fast_key = jax.random.split(key, 3)
    share = 0.5
    chosen = jax.random.uniform(pick_key, (HEADS,), jnp.float32) < share
    slow_rate = jax.random.uniform(slow_key, (HEADS,), jnp.float32, jnp.log(0.2 / TOKENS), jnp.log(1.5 / TOKENS))
    fast_rate = jax.random.uniform(fast_key, (HEADS,), jnp.float32, jnp.log(1.0 / 60.0), jnp.log(1.0 / 20.0))
    return jnp.where(chosen, slow_rate, fast_rate).astype(jnp.float32)


def block_levels(key, dims, cuts, least, top_value):
    def one(axis_at, shards_of):
        steps = jax.random.uniform(jax.random.fold_in(jax.random.fold_in(key, 6), axis_at), (shards_of,), jnp.float32, least / len(cuts), top_value / len(cuts))
        return jnp.repeat(jnp.exp(steps), dims[axis_at] // shards_of).reshape((-1,) + (1,) * (len(dims) - axis_at - 1))

    loudness = one(*cuts[0])
    for cut in cuts[1:]:
        loudness = loudness * one(*cut)
    return loudness


def noise(rng, dims, scale, most, cuts=(), held_as=jnp.bfloat16):
    level = block_levels(rng, dims, cuts, -0.22, 0.18) if cuts else 1.0
    values = jax.random.normal(rng, dims, jnp.float32) * scale * level
    return jnp.minimum(jnp.maximum(values, -most), most).astype(held_as)


def setup_inputs(seed: int = 0) -> dict:
    arg_keys = jax.random.split(jax.random.key(seed), 10)
    return {
        "x_proj": noise(arg_keys[0], (TOKENS, INNER), 1.0, 6.0, ((0, 512),)),
        "z_gate": noise(arg_keys[1], (TOKENS, INNER), 1.0, 6.0, ((0, 512),)),
        "out_grad": noise(arg_keys[2], (TOKENS, INNER), 1.0, 6.0, ((0, 512),)),
        "b_proj": noise(arg_keys[3], (TOKENS, PROJ_BC), ((0.6 * STATE) ** -0.25 * (20 * TOKENS) ** -0.125), 1.0, ((0, 512),)),
        "c_proj": noise(arg_keys[4], (TOKENS, PROJ_BC), ((0.6 * STATE) ** -0.25 * (20 * TOKENS) ** -0.125), 1.0, ((0, 512),)),
        "dt_raw": noise(arg_keys[5], (TOKENS, HEADS), 0.5, 3.0, ((0, 512),)),
        "dt_bias": jnp.clip(jax.random.uniform(arg_keys[6], (HEADS,), jnp.float32, -0.5, 0.5) * block_levels(arg_keys[6], (HEADS,), ((0, 8),), -0.4, 0.0), -0.5, 0.5),
        "a_log": draw_a_log(jax.random.fold_in(arg_keys[9], 71), 0),
        "d_skip": jnp.clip(0.5 + 1.0 * jax.random.uniform(arg_keys[8], (HEADS,), jnp.float32) ** block_levels(arg_keys[8], (HEADS,), ((0, 8),), -0.2, 0.2), 0.5, 1.5),
    }


PRECISE = lax.Precision.HIGHEST

def block_forward(x_heads, b_heads, c_heads, raw_steps, step_bias, decay_log, skip_gain, carry_state):
    step_size = jax.nn.softplus(raw_steps + step_bias)
    cumlog = jnp.cumsum(-jnp.exp(decay_log) * step_size, axis=0)
    across = jnp.transpose(cumlog, (1, 2, 0))
    step_cols = jnp.transpose(step_size, (1, 2, 0))
    length = x_heads.shape[0]
    positions = jnp.arange(length)
    causal = positions[:, None] >= positions[None, :]
    spread = jnp.where(causal[None, None], across[:, :, :, None] - across[:, :, None, :], -jnp.inf)
    affinity = jnp.einsum('tgn,sgn->gts', c_heads, b_heads, precision=PRECISE)
    scores = jnp.exp(spread) * affinity[:, None] * step_cols[:, :, None, :]
    output = jnp.einsum('gjts,sgjp->tgjp', scores, x_heads, precision=PRECISE)
    carried = jnp.einsum('tgn,gjpn->tgjp', c_heads, carry_state, precision=PRECISE)
    output = output + jnp.exp(cumlog)[..., None] * carried
    output = output + skip_gain[..., None] * x_heads
    weights = jnp.exp(cumlog[-1][None] - cumlog) * step_size
    ending = jnp.einsum('tgn,tgjp->gjpn', b_heads, weights[..., None] * x_heads, precision=PRECISE)
    ending = ending + jnp.exp(cumlog[-1])[..., None, None] * carry_state
    return (output, ending)

def silu_slope(signal):
    squash = jax.nn.sigmoid(signal)
    return squash * (1.0 + signal * (1.0 - squash))

def reference(x_proj, z_gate, out_grad, b_proj, c_proj, dt_raw, dt_bias, a_log, d_skip):
    total = x_proj.shape[0]
    per_group = HEADS // GROUPS
    blocks = total // SEQ_DEV

    def heads_view(array):
        return array.astype(jnp.float32).reshape(total, GROUPS, per_group, HEAD_DIM)
    x_all = heads_view(x_proj)
    z_all = heads_view(z_gate)
    cot_all = heads_view(out_grad)
    gated_low = (cot_all * jax.nn.silu(z_all)).astype(jnp.bfloat16)
    gated_all = lax.optimization_barrier(gated_low).astype(jnp.float32)
    b_all = b_proj.astype(jnp.float32).reshape(total, GROUPS, STATE)
    c_all = c_proj.astype(jnp.float32).reshape(total, GROUPS, STATE)
    raw_all = dt_raw.astype(jnp.float32).reshape(total, GROUPS, per_group)
    bias_all = dt_bias.reshape(GROUPS, per_group)
    alog_all = a_log.reshape(GROUPS, per_group)
    skip_all = d_skip.reshape(GROUPS, per_group)

    def one_group(pieces):
        x_one, b_one, c_one, raw_one, bias_one, alog_one, skip_one, gated_one = pieces

        def whole(x_in, b_in, c_in, raw_in, bias_in, alog_in, skip_in):

            def advance(carry_state, block_data):
                x_blk, b_blk, c_blk, raw_blk = block_data
                result, next_state = block_forward(x_blk, b_blk, c_blk, raw_blk, bias_in, alog_in, skip_in, carry_state)
                return (next_state, result)
            start = jnp.zeros((1, per_group, HEAD_DIM, STATE), jnp.float32)
            block_data = (x_in.reshape(blocks, SEQ_DEV, 1, per_group, HEAD_DIM), b_in.reshape(blocks, SEQ_DEV, 1, STATE), c_in.reshape(blocks, SEQ_DEV, 1, STATE), raw_in.reshape(blocks, SEQ_DEV, 1, per_group))
            _, results = lax.scan(advance, start, block_data)
            return results.reshape(total, 1, per_group, HEAD_DIM)
        primal, pullback = jax.vjp(whole, x_one[:, None], b_one[:, None], c_one[:, None], raw_one[:, None], bias_one[None], alog_one[None], skip_one[None])
        gradients = pullback(gated_one[:, None])
        return (primal[:, 0],) + tuple(gradients)
    outcome = lax.map(one_group, (jnp.transpose(x_all, (1, 0, 2, 3)), jnp.transpose(b_all, (1, 0, 2)), jnp.transpose(c_all, (1, 0, 2)), jnp.transpose(raw_all, (1, 0, 2)), bias_all, alog_all, skip_all, jnp.transpose(gated_all, (1, 0, 2, 3))))
    y_all = jnp.transpose(outcome[0], (1, 0, 2, 3))
    saved_low = y_all.astype(jnp.bfloat16)
    restored = lax.optimization_barrier(saved_low).astype(jnp.float32)
    grad_z = (cot_all * restored * silu_slope(z_all)).astype(jnp.bfloat16).reshape(total, INNER)
    grad_x = jnp.transpose(outcome[1][:, :, 0], (1, 0, 2, 3)).reshape(total, INNER).astype(jnp.bfloat16)
    grad_b = jnp.transpose(outcome[2][:, :, 0], (1, 0, 2)).reshape(total, PROJ_BC).astype(jnp.bfloat16)
    grad_c = jnp.transpose(outcome[3][:, :, 0], (1, 0, 2)).reshape(total, PROJ_BC).astype(jnp.bfloat16)
    grad_dt = jnp.transpose(outcome[4][:, :, 0], (1, 0, 2)).reshape(total, HEADS).astype(jnp.bfloat16)
    grad_bias = outcome[5].reshape(HEADS)
    grad_alog = outcome[6].reshape(HEADS)
    grad_dskip = outcome[7].reshape(HEADS)
    return (grad_x, grad_z, grad_b, grad_c, grad_dt, grad_bias, grad_alog, grad_dskip)
```

```python
import functools

import jax
import jax.numpy as jnp
from jax import lax
from jax.experimental import pallas as pl
from jax.experimental.pallas import tpu as pltpu
from jax.sharding import PartitionSpec as P

ROW = 8
TOK = 16
STATE = 128
LANES = 128
HALF = 64
EARLY = 8

F32 = jnp.float32
BF16 = jnp.bfloat16
MESH = pl.DeviceIdType.MESH


def mm(a, b, ca, cb):
    return lax.dot_general(a, b, (((ca,), (cb,)), ((), ())), preferred_element_type=F32)


def mm_exact(a, b):
    return lax.dot_general(
        a,
        b,
        (((1,), (0,)), ((), ())),
        precision=lax.Precision.HIGHEST,
        preferred_element_type=F32,
    )


def loop(low, high, body):
    def step(i, carry):
        body(i)
        return carry

    lax.fori_loop(low, high, step, 0)


def bytes_wait(ref, sem):
    pltpu.make_async_copy(ref, ref, sem).wait()


def kernel(
    sizes,
    x_ref, z_ref, og_ref, b_ref, c_ref, dt_ref, bias_ref, alog_ref, skip_ref,
    gx_ref, gz_ref, gb_ref, gc_ref, gdt_ref, sums_ref,
    sxg, rxg, sbc, rzb, rbc, sdt, rdt, ysend, yrecv, out, rout, sdbc, rdbc, sgd, rgd, szo, rzo,
    ssy, rsy, ssr, rsr,
    slope, turn, cols, ecol, wcol, eg, wx, st_s, st_a, hb, gb16, y_in, dx_in, dc_in, db_in,
    ds0, dla0, rho, kap, cterm, skipsum,
    zb_send, zb_recv, xg_send, xg_recv, bc_send, bc_recv, dt_send, dt_recv, y_send, y_recv,
    out_send, out_recv, db_send, db_recv, gd_send, gd_recv, zo_send, zo_recv,
    sy_send, sy_recv, sr_send, sr_recv,
):
    slabs, row, zs, heads = sizes
    length = zs * TOK
    per = 2 * row
    seq, z = lax.axis_index("seq"), lax.axis_index("head")
    y, r = lax.div(seq, row), lax.rem(seq, row)
    mine = pl.ds(pl.multiple_of(z * TOK, TOK), TOK)

    def at(row_to, z_to):
        return (y * row + row_to, z_to)

    def send(src, dst, send_sem, recv_sem, device):
        pltpu.make_async_remote_copy(
            src_ref=src,
            dst_ref=dst,
            send_sem=send_sem,
            recv_sem=recv_sem,
            device_id=device,
            device_id_type=MESH,
        ).start()

    barrier = pltpu.get_barrier_semaphore()

    def greet(i):
        there = at(lax.rem(r + lax.div(i, zs), row), lax.rem(z + lax.rem(i, zs), zs))
        pl.semaphore_signal(barrier, inc=1, device_id=there, device_id_type=MESH)

    def greet_slab(i):
        there = (lax.rem(y + i, slabs) * row + r, z)
        pl.semaphore_signal(barrier, inc=1, device_id=there, device_id_type=MESH)

    loop(1, row * zs, greet)
    loop(1, slabs, greet_slab)

    for k in range(zs):
        sbc[k, 0] = b_ref[:, k * STATE : (k + 1) * STATE]
        sbc[k, 1] = c_ref[:, k * STATE : (k + 1) * STATE]
        sbc[k, 2, :, 0:heads] = dt_ref[...]

    def gate(d):
        span = pl.ds(pl.multiple_of(d * LANES, LANES), LANES)
        zf, of = z_ref[:, span].astype(F32), og_ref[:, span].astype(F32)
        s = jax.nn.sigmoid(zf)
        sxg[d, 0] = x_ref[:, span]
        sxg[d, 1] = (of * (zf * s)).astype(BF16)
        slope[:, span] = of * (s * (1.0 + zf * (1.0 - s)))

    loop(0, row * zs, gate)
    pl.semaphore_wait(barrier, row * zs - 1 + slabs - 1)

    pltpu.make_async_copy(sbc.at[z], rzb.at[:, mine, :], zb_recv).start()

    def send_zb(i):
        to = lax.rem(z + i, zs)
        send(sbc.at[to], rzb.at[:, mine, :], zb_send, zb_recv, at(r, to))

    loop(1, zs, send_zb)

    pltpu.make_async_copy(sxg.at[z * row + r], rxg.at[r, :, mine, :], xg_recv.at[r]).start()

    def send_xg(i):
        r_to, z_to = lax.rem(r + lax.div(i, zs), row), lax.rem(z + lax.rem(i, zs), zs)
        send(
            sxg.at[z_to * row + r_to], rxg.at[r, :, mine, :], xg_send, xg_recv.at[r], at(r_to, z_to)
        )

    loop(1, 2 * zs, send_xg)

    bytes_wait(rzb, zb_recv)
    pltpu.make_async_copy(rzb.at[pl.ds(0, 2)], rbc.at[r], bc_recv.at[r]).start()

    def send_bc(i):
        to = lax.rem(r + i, row)
        send(rzb.at[pl.ds(0, 2)], rbc.at[r], bc_send, bc_recv.at[r], at(to, z))

    loop(1, row, send_bc)

    turn[...] = jnp.transpose(rzb[2].astype(F32)[:, 0:heads])
    raw = turn[pl.ds(pl.multiple_of(z * per, per), per), :]
    head_at = lax.broadcasted_iota(jnp.int32, (per, length), 0)
    token_at = lax.broadcasted_iota(jnp.int32, (per, length), 1)
    bias = jnp.zeros((per, length), F32)
    rate = jnp.zeros((per, length), F32)
    for h in range(per):
        bias = jnp.where(head_at == h, bias_ref[h], bias)
        rate = jnp.where(head_at == h, alog_ref[h], rate)
    pre = raw + bias
    step = jnp.maximum(pre, 0.0) + jnp.log1p(jnp.exp(-jnp.abs(pre)))
    squash = jax.nn.sigmoid(pre)
    decay = -jnp.exp(rate) * step
    cum = decay
    reach = 1
    while reach < length:
        cum = cum + jnp.where(token_at >= reach, pltpu.roll(cum, reach, 1), 0.0)
        reach *= 2
    for d in range(row):
        pair = slice(2 * d, 2 * d + 2)
        sdt[d] = jnp.concatenate([step[pair], cum[pair], squash[pair], decay[pair]], axis=0)
    pltpu.make_async_copy(sdt.at[r], rdt.at[r], dt_recv.at[r]).start()

    def send_dt(i):
        to = lax.rem(r + i, row)
        send(sdt.at[to], rdt.at[r], dt_send, dt_recv.at[r], at(to, z))

    loop(1, row, send_dt)
    loop(2 * zs, row * zs, send_xg)

    lane = lax.broadcasted_iota(jnp.int32, (1, LANES), 1)
    first = lane < HALF
    sel = [first.astype(F32), 1.0 - first.astype(F32)]
    skip = jnp.where(first, skip_ref[2 * r], skip_ref[2 * r + 1])
    at_row = lax.broadcasted_iota(jnp.int32, (length, length), 0)
    at_col = lax.broadcasted_iota(jnp.int32, (length, length), 1)
    causal = at_row >= at_col
    before = (at_row < at_col).astype(F32)
    sel_at = lax.broadcasted_iota(jnp.int32, (16, LANES), 0)
    sel_lane = lax.broadcasted_iota(jnp.int32, (16, LANES), 1)
    pick = jnp.where(sel_at == lax.div(sel_lane, HALF), 1.0, 0.0)

    def last_decay(c):
        rows = rdt[c]
        return jnp.exp(jnp.where(first, rows[2:3, length - 1 :], rows[3:4, length - 1 :]))

    def outer(c):
        rows = rdt[c]
        across = jnp.transpose(rows)
        cols[c] = across
        up = jnp.where(first, across[:, 2:3], across[:, 3:4])
        end = jnp.where(first, rows[2:3, length - 1 :], rows[3:4, length - 1 :])
        size = jnp.where(first, across[:, 0:1], across[:, 1:2])
        e = jnp.exp(up)
        w = jnp.exp(end - up) * size
        ecol[c] = e
        wcol[c] = w
        grown = (w * rxg[c, 0].astype(F32)).astype(BF16)
        faded = (e * rxg[c, 1].astype(F32)).astype(BF16)
        wx[c] = grown
        eg[c] = faded
        st_s[c] = mm(rbc[c, 0], grown, 0, 0)
        st_a[c] = mm(rbc[c, 1], faded, 0, 0)

    def inner(c):
        xs, gs, bs, cs = rxg[c, 0], rxg[c, 1], rbc[c, 0], rbc[c, 1]
        xf, gf = xs.astype(F32), gs.astype(F32)
        across = cols[c]
        aff = mm(cs, bs, 1, 1)
        y_sum = skip * xf
        dx_sum = skip * gf
        pulls = jnp.zeros((length, length), F32)
        for j in range(2):
            x_j, g_j = (xf * sel[j]).astype(BF16), (gf * sel[j]).astype(BF16)
            size = rdt[c, j : j + 1, :]
            fall = across[:, 2 + j : 3 + j] - rdt[c, 2 + j : 3 + j, :]
            e = jnp.where(causal, jnp.exp(fall), 0.0)
            dots = mm(g_j, xs, 1, 1)
            ea = e * aff
            score = (ea * size).astype(BF16)
            k0 = ea * dots
            ds0[c, j : j + 1, :] = jnp.sum(k0, axis=0, keepdims=True)
            crossing = mm((k0 * size).astype(BF16), before.astype(BF16), 1, 0)
            dla0[c, j : j + 1, :] = jnp.sum(
                jnp.where(causal, crossing, 0.0), axis=0, keepdims=True
            )
            pulls = pulls + e * dots * size
            y_sum = y_sum + mm(score, x_j, 1, 0)
            dx_sum = dx_sum + mm(score, g_j, 0, 0)
        pulls = pulls.astype(BF16)
        y_in[c] = y_sum
        dx_in[c] = dx_sum
        dc_in[c] = mm(pulls, bs, 1, 0)
        db_in[c] = mm(pulls, cs, 0, 0)
        skipsum[...] = skipsum[...] + jnp.sum(xf * gf, axis=0, keepdims=True)

    skipsum[...] = jnp.zeros_like(skipsum)

    def arrive(k):
        c = lax.rem(r + row - k, row)
        bytes_wait(rbc.at[c], bc_recv.at[c])
        bytes_wait(rdt.at[c], dt_recv.at[c])
        bytes_wait(rxg.at[c], xg_recv.at[c])
        outer(c)

        @pl.when(k < EARLY)
        def _():
            inner(c)

    loop(0, row, arrive)

    state = jnp.zeros((STATE, LANES), F32)
    back = jnp.zeros((STATE, LANES), F32)
    keep = jnp.ones((1, LANES), F32)
    for c in range(row):
        fade = last_decay(c)
        keep = keep * fade
        state = fade * state + st_s[c]
    for c in reversed(range(row)):
        back = last_decay(c) * back + st_a[c]
    high = keep.astype(BF16).astype(F32)
    mid = (keep - high).astype(BF16).astype(F32)
    low = keep - high - mid
    tail_at = lax.broadcasted_iota(jnp.int32, (16, LANES), 0)
    tail = jnp.where(tail_at == 0, high, jnp.where(tail_at == 1, mid, low)).astype(BF16)
    ysend[0, 0:STATE] = state.astype(BF16)
    ysend[1, 0:STATE] = back.astype(BF16)
    ysend[0, STATE : STATE + 16] = tail
    ysend[1, STATE : STATE + 16] = tail

    def send_state(i):
        wrapped = lax.div(y + i, slabs)
        send(
            ysend.at[wrapped],
            yrecv.at[y],
            y_send,
            y_recv.at[y],
            (lax.rem(y + i, slabs) * row + r, z),
        )

    loop(1, slabs, send_state)

    def late(k):
        inner(lax.rem(r + row - k, row))

    loop(EARLY, row, late)

    def await_state(i):
        source = lax.rem(y + i, slabs)
        bytes_wait(yrecv.at[source], y_recv.at[source])

    loop(1, slabs, await_state)

    state = jnp.zeros((STATE, LANES), F32)
    back = jnp.zeros((STATE, LANES), F32)
    for i in reversed(range(1, slabs)):
        for ahead in (False, True):
            source = lax.rem(y + i if ahead else y + slabs - i, slabs)
            counts = (y + i < slabs) if ahead else (y >= i)
            ends = yrecv[source, STATE : STATE + 16].astype(F32)
            fade = ends[0:1] + ends[1:2] + ends[2:3]
            part = yrecv[source, 0:STATE].astype(F32)
            if ahead:
                back = jnp.where(counts, fade * back + part, back)
            else:
                state = jnp.where(counts, fade * state + part, state)
    for c in range(row):
        hb[c] = state.astype(BF16)
        here = st_s[c]
        st_s[c] = state
        state = last_decay(c) * state + here
    for c in reversed(range(row)):
        gb16[c] = back.astype(BF16)
        fade = last_decay(c)
        over = fade * jnp.sum(st_s[c] * back, axis=0, keepdims=True)
        cterm[c] = jnp.broadcast_to(
            jnp.sum(pick[0:8] * over, axis=1, keepdims=True), (8, length)
        )
        back = fade * back + st_a[c]

    pick16 = pick.astype(BF16)

    def finish(k):
        c = lax.rem(r + k, row)
        xs, gs, bs, cs = rxg[c, 0], rxg[c, 1], rbc[c, 0], rbc[c, 1]
        h, g = hb[c], gb16[c]
        dc = dc_in[c] + mm(eg[c], h, 1, 1)
        db = db_in[c] + mm(wx[c], g, 1, 1)
        sdbc[c, 0] = db.astype(BF16)
        sdbc[c, 1] = dc.astype(BF16)

        @pl.when(k > 0)
        def _():
            send(sdbc.at[c], rdbc.at[r], db_send, db_recv.at[r], at(c, z))

        yi = ecol[c] * mm(cs, h, 1, 0)
        bi = wcol[c] * mm(bs, g, 1, 0)
        out[c, 0] = (dx_in[c] + bi).astype(BF16)
        out[c, 1] = (y_in[c] + yi).astype(BF16)
        there = pl.ds(pl.multiple_of((z * row + r) * LANES, LANES), LANES)

        @pl.when(k == 0)
        def _():
            pltpu.make_async_copy(sdbc.at[c], rdbc.at[r], db_recv.at[r]).start()
            pltpu.make_async_copy(out.at[c, :, mine, :], rout.at[:, :, there], out_recv).start()

        @pl.when(k > 0)
        def _():
            send(out.at[c, :, mine, :], rout.at[:, :, there], out_send, out_recv, at(c, z))

        def send_out(i):
            z_to = lax.rem(z + i, zs)
            part = pl.ds(pl.multiple_of(z_to * TOK, TOK), TOK)
            send(out.at[c, :, part, :], rout.at[:, :, there], out_send, out_recv, at(c, z_to))

        loop(1, zs, send_out)
        rho[c] = mm(pick16, (gs.astype(F32) * yi).astype(BF16), 1, 1)[0:8]
        kap[c] = mm(pick16, (xs.astype(F32) * bi).astype(BF16), 1, 1)[0:8]

    loop(0, row, finish)

    flat = (row * 8, length)
    dla = (
        dla0[...].reshape(flat)
        + mm_exact(rho[...].reshape(flat), causal.astype(F32))
        + mm_exact(kap[...].reshape(flat), before)
        + cterm[...].reshape(flat)
    )
    parts = [rdt[c] for c in range(row)]
    steps = jnp.concatenate(parts, axis=0)
    squashes = jnp.concatenate([pltpu.roll(p, 4, 0) for p in parts], axis=0)
    decays = jnp.concatenate([pltpu.roll(p, 2, 0) for p in parts], axis=0)
    which = lax.rem(lax.broadcasted_iota(jnp.int32, flat, 0), 8)
    rates = jnp.exp(jnp.where(which == 0, alog_ref[2 * r], alog_ref[2 * r + 1]))
    dsteps = ds0[...].reshape(flat) + kap[...].reshape(flat) / steps - rates * dla
    draws = jnp.where(which < 2, dsteps * squashes, 0.0)
    dlogs = jnp.where(which < 2, dla * decays, 0.0)
    sgd[...] = draws.reshape(row, 8, length)
    pltpu.make_async_copy(sgd.at[r], rgd.at[r], gd_recv.at[r]).start()

    def send_gd(i):
        to = lax.rem(r + i, row)
        send(sgd.at[to], rgd.at[r], gd_send, gd_recv.at[r], at(to, z))

    loop(1, row, send_gd)

    sum_at = lax.broadcasted_iota(jnp.int32, (8, LANES), 0)
    sum_lane = lax.broadcasted_iota(jnp.int32, (8, LANES), 1)
    sums = jnp.zeros((8, LANES), F32)
    for j in range(2):
        totals = (
            jnp.sum(jnp.where(which == j, draws, 0.0)),
            jnp.sum(jnp.where(which == j, dlogs, 0.0)),
            jnp.sum(skipsum[...] * sel[j]),
        )
        for q in range(3):
            place = (sum_at == q) & (sum_lane == 2 * r + j)
            sums = jnp.where(place, totals[q], sums)
    ssy[...] = sums
    pltpu.make_async_copy(ssy, rsy.at[y], sy_recv).start()

    def send_sy(i):
        send(ssy, rsy.at[y], sy_send, sy_recv, (lax.rem(y + i, slabs) * row + r, z))

    loop(1, slabs, send_sy)

    loop(0, row, lambda c: bytes_wait(rdbc.at[c], db_recv.at[c]))
    for q in range(2):
        total = rdbc[0, q].astype(F32)
        for c in range(1, row):
            total = total + rdbc[c, q].astype(F32)
        szo[q] = total.astype(BF16)
    loop(0, row, lambda c: bytes_wait(rgd.at[c], gd_recv.at[c]))
    turn[...] = jnp.zeros_like(turn)
    turn[pl.ds(pl.multiple_of(z * per, per), per), :] = jnp.concatenate(
        [rgd[c][0:2] for c in range(row)], axis=0
    )
    szo[2, :, 0:heads] = jnp.transpose(turn[...]).astype(BF16)
    pltpu.make_async_copy(szo.at[:, mine, :], rzo.at[z], zo_recv).start()

    def send_zo(i):
        to = lax.rem(z + i, zs)
        part = pl.ds(pl.multiple_of(to * TOK, TOK), TOK)
        send(szo.at[:, part, :], rzo.at[z], zo_send, zo_recv, at(r, to))

    loop(1, zs, send_zo)

    bytes_wait(rsy, sy_recv)
    total = rsy[0]
    for i in range(1, slabs):
        total = total + rsy[i]
    ssr[...] = total
    pltpu.make_async_copy(ssr, rsr.at[r], sr_recv).start()

    def send_sr(i):
        send(ssr, rsr.at[r], sr_send, sr_recv, at(lax.rem(r + i, row), z))

    loop(1, row, send_sr)

    bytes_wait(rout, out_recv)
    gx_ref[...] = rout[0]

    def gate_back(d):
        span = pl.ds(pl.multiple_of(d * LANES, LANES), LANES)
        gz_ref[:, span] = (slope[:, span] * rout[1, :, span].astype(F32)).astype(BF16)

    loop(0, row * zs, gate_back)

    bytes_wait(rzo, zo_recv)
    total = jnp.zeros((TOK, heads), F32)
    for k in range(zs):
        gb_ref[:, k * STATE : (k + 1) * STATE] = rzo[k, 0]
        gc_ref[:, k * STATE : (k + 1) * STATE] = rzo[k, 1]
        total = total + rzo[k, 2, :, 0:heads].astype(F32)
    gdt_ref[...] = total.astype(BF16)
    bytes_wait(rsr, sr_recv)
    total = rsr[0]
    for i in range(1, row):
        total = total + rsr[i]
    sums_ref[...] = total

    bytes_wait(sbc.at[pl.ds(0, zs - 1)], zb_send)
    bytes_wait(sxg.at[pl.ds(0, row * zs - 1)], xg_send)
    bytes_wait(rbc.at[pl.ds(0, row - 1)], bc_send)
    bytes_wait(sdt.at[pl.ds(0, row - 1)], dt_send)
    bytes_wait(yrecv.at[pl.ds(0, slabs - 1)], y_send)
    bytes_wait(sxg.at[pl.ds(0, row * zs - 1)], out_send)
    bytes_wait(rdbc.at[pl.ds(0, row - 1)], db_send)
    bytes_wait(sgd.at[pl.ds(0, row - 1)], gd_send)
    bytes_wait(rzo.at[pl.ds(0, zs - 1)], zo_send)
    bytes_wait(rsy.at[pl.ds(0, slabs - 1)], sy_send)
    bytes_wait(rsr.at[pl.ds(0, row - 1)], sr_send)


def shards(row, x_proj, z_gate, out_grad, b_proj, c_proj, dt_raw, dt_bias, a_log, d_skip):
    zs = lax.axis_size("head")
    slabs = lax.axis_size("seq") // row
    heads = 2 * row * zs
    length = zs * TOK
    inner = heads * HALF

    def vmem(*shape, dtype=BF16):
        return pltpu.VMEM(shape, dtype)

    square = (row, length, LANES)
    states = (row, STATE, LANES)
    scratch = [
        vmem(row * zs, 2, TOK, LANES),
        vmem(row, 2, length, LANES),
        vmem(zs, 3, TOK, STATE),
        vmem(3, length, STATE),
        vmem(row, 2, length, STATE),
        vmem(row, 8, length, dtype=F32),
        vmem(row, 8, length, dtype=F32),
        vmem(2, STATE + 16, LANES),
        vmem(slabs, STATE + 16, LANES),
        vmem(row, 2, length, LANES),
        vmem(2, TOK, inner),
        vmem(row, 2, length, STATE),
        vmem(row, 2, length, STATE),
        vmem(row, 8, length, dtype=F32),
        vmem(row, 8, length, dtype=F32),
        vmem(3, length, STATE),
        vmem(zs, 3, TOK, STATE),
        vmem(8, LANES, dtype=F32),
        vmem(slabs, 8, LANES, dtype=F32),
        vmem(8, LANES, dtype=F32),
        vmem(row, 8, LANES, dtype=F32),
        vmem(TOK, inner, dtype=F32),
        vmem(heads, length, dtype=F32),
        vmem(row, length, 8, dtype=F32),
        vmem(*square, dtype=F32),
        vmem(*square, dtype=F32),
        vmem(*square),
        vmem(*square),
        vmem(*states, dtype=F32),
        vmem(*states, dtype=F32),
        vmem(*states),
        vmem(*states),
        vmem(*square, dtype=F32),
        vmem(*square, dtype=F32),
        vmem(*square, dtype=F32),
        vmem(*square, dtype=F32),
        vmem(row, 8, length, dtype=F32),
        vmem(row, 8, length, dtype=F32),
        vmem(row, 8, length, dtype=F32),
        vmem(row, 8, length, dtype=F32),
        vmem(row, 8, length, dtype=F32),
        vmem(1, LANES, dtype=F32),
    ]
    one, many = pltpu.SemaphoreType.DMA, lambda n: pltpu.SemaphoreType.DMA((n,))
    semaphores = [
        one, one,
        one, many(row),
        one, many(row),
        one, many(row),
        one, many(slabs),
        one, one,
        one, many(row),
        one, many(row),
        one, one,
        one, one,
        one, one,
    ]
    in_vmem = pl.BlockSpec(memory_space=pltpu.VMEM)
    in_smem = pl.BlockSpec(memory_space=pltpu.SMEM)
    like = jax.ShapeDtypeStruct
    results = pl.pallas_call(
        functools.partial(kernel, (slabs, row, zs, heads)),
        out_shape=[
            like((TOK, inner), BF16),
            like((TOK, inner), BF16),
            like((TOK, zs * STATE), BF16),
            like((TOK, zs * STATE), BF16),
            like((TOK, heads), BF16),
            like((8, LANES), F32),
        ],
        in_specs=[in_vmem] * 6 + [in_smem] * 3,
        out_specs=[in_vmem] * 6,
        scratch_shapes=scratch + semaphores,
        compiler_params=pltpu.CompilerParams(
            collective_id=0, has_side_effects=True, vmem_limit_bytes=40 * 2**20
        ),
        name="scan_backward",
    )(x_proj, z_gate, out_grad, b_proj, c_proj, dt_raw, dt_bias, a_log, d_skip)
    per = 2 * row
    sums = results[5]
    return (*results[:5], sums[0, :per], sums[1, :per], sums[2, :per])


def solution(mesh, row=ROW):
    tokens = P(("seq", "head"), None)
    return jax.shard_map(
        functools.partial(shards, row),
        mesh=mesh,
        in_specs=(tokens,) * 6 + (P("head"),) * 3,
        out_specs=(tokens,) * 5 + (P("head"),) * 3,
        check_vma=False,
    )
```

```python
import functools

import jax
import jax.numpy as jnp
from jax import lax
from jax.experimental import pallas as pl
from jax.experimental.pallas import tpu as pltpu
from jax.sharding import PartitionSpec as P

ROW = 8
TOK = 16
STATE = 128
LANES = 128
HALF = 64
AHEAD = 4

F32 = jnp.float32
BF16 = jnp.bfloat16
MESH = pl.DeviceIdType.MESH


def mm(a, b, ca, cb):
    return lax.dot_general(a, b, (((ca,), (cb,)), ((), ())), preferred_element_type=F32)


def mm_exact(a, b):
    return lax.dot_general(
        a,
        b,
        (((1,), (0,)), ((), ())),
        precision=lax.Precision.HIGHEST,
        preferred_element_type=F32,
    )


def loop(low, high, body):
    def step(i, carry):
        body(i)
        return carry

    lax.fori_loop(low, high, step, 0)


def bytes_wait(ref, sem):
    pltpu.make_async_copy(ref, ref, sem).wait()


def kernel(
    sizes,
    x_hbm, z_hbm, og_hbm, b_hbm, c_hbm, dt_hbm, bias_hbm, alog_hbm, skip_hbm,
    inner_ref, outer_ref, gdt_ref, sums_ref,
    x_ref, z_ref, og_ref, b_ref, c_ref, dt_ref, bias_ref, alog_ref, skip_ref,
    sg, rx, rg, sbc, rzb, rb, rc, sdt, rdt, ssend, asend, srecv, arecv, sy, sdx, ry, rdx,
    sdb, sdc, rdb, rdc, sgd, rgd, szo, rzo, ssy, rsy, ssr, rsr,
    slope, turn, cols, ecol, wcol, eg, wx, st_s, st_a, hb, affs, decs, scores,
    y_in, dx_in, db_in, ds0, dla0, rho, kap, cterm, skipsum,
    zb_send, zb_recv, x_send, x_recv, g_send, g_recv, b_send, b_recv, c_send, c_recv,
    dt_send, dt_recv, s_send, s_recv, a_send, a_recv, y_send, y_recv, dx_send, dx_recv,
    db_send, db_recv, dc_send, dc_recv, gd_send, gd_recv, zo_send, zo_recv,
    sy_send, sy_recv, sr_send, sr_recv, load,
):
    slabs, row, zs, heads = sizes
    length = zs * TOK
    per = 2 * row
    seq, z = lax.axis_index("seq"), lax.axis_index("head")
    y, r = lax.div(seq, row), lax.rem(seq, row)
    mine = pl.ds(pl.multiple_of(z * TOK, TOK), TOK)

    def at(row_to, z_to):
        return (y * row + row_to, z_to)

    def other(i):
        return lax.rem(r + lax.div(i, zs), row), lax.rem(z + lax.rem(i, zs), zs)

    def lanes_of(d):
        return pl.ds(pl.multiple_of(d * LANES, LANES), LANES)

    def tokens_of(k):
        return pl.ds(pl.multiple_of(k * TOK, TOK), TOK)

    def send(src, dst, send_sem, recv_sem, device):
        pltpu.make_async_remote_copy(
            src_ref=src,
            dst_ref=dst,
            send_sem=send_sem,
            recv_sem=recv_sem,
            device_id=device,
            device_id_type=MESH,
        ).start()

    def keep(src, dst, recv_sem):
        pltpu.make_async_copy(src, dst, recv_sem).start()

    loads = [
        pltpu.make_async_copy(there, here, load.at[i])
        for i, (there, here) in enumerate(
            (
                (b_hbm, b_ref),
                (c_hbm, c_ref),
                (dt_hbm, dt_ref),
                (x_hbm, x_ref),
                (z_hbm, z_ref),
                (og_hbm, og_ref),
                (bias_hbm, bias_ref),
                (alog_hbm, alog_ref),
                (skip_hbm, skip_ref),
            )
        )
    ]
    for copy in loads:
        copy.start()

    barrier = pltpu.get_barrier_semaphore()

    def greet(i):
        pl.semaphore_signal(barrier, inc=1, device_id=at(*other(i)), device_id_type=MESH)

    def greet_slab(i):
        there = (lax.rem(y + i, slabs) * row + r, z)
        pl.semaphore_signal(barrier, inc=1, device_id=there, device_id_type=MESH)

    loop(1, row * zs, greet)
    loop(1, slabs, greet_slab)

    for copy in loads[:3]:
        copy.wait()
    for k in range(zs):
        sbc[k, 0] = b_ref[:, k * STATE : (k + 1) * STATE]
        sbc[k, 1] = c_ref[:, k * STATE : (k + 1) * STATE]
        sbc[k, 2, :, 0:heads] = dt_ref[...]
    loads[3].wait()
    pl.semaphore_wait(barrier, row * zs - 1 + slabs - 1)

    keep(sbc.at[z], rzb.at[:, mine, :], zb_recv)

    def send_zb(i):
        to = lax.rem(z + i, zs)
        send(sbc.at[to], rzb.at[:, mine, :], zb_send, zb_recv, at(r, to))

    loop(1, zs, send_zb)

    keep(x_ref.at[:, lanes_of(z * row + r)], rx.at[r, mine, :], x_recv.at[r])

    def send_x(i):
        r_to, z_to = other(i)
        send(
            x_ref.at[:, lanes_of(z_to * row + r_to)],
            rx.at[r, mine, :],
            x_send,
            x_recv.at[r],
            at(r_to, z_to),
        )

    loop(1, AHEAD * zs, send_x)

    bytes_wait(rzb, zb_recv)
    keep(rzb.at[0], rb.at[r], b_recv.at[r])
    keep(rzb.at[1], rc.at[r], c_recv.at[r])

    def send_b(i):
        to = lax.rem(r + i, row)
        send(rzb.at[0], rb.at[r], b_send, b_recv.at[r], at(to, z))

    loop(1, row, send_b)

    for copy in loads[4:]:
        copy.wait()
    turn[...] = jnp.transpose(rzb[2].astype(F32)[:, 0:heads])
    raw = turn[pl.ds(pl.multiple_of(z * per, per), per), :]
    head_at = lax.broadcasted_iota(jnp.int32, (per, length), 0)
    token_at = lax.broadcasted_iota(jnp.int32, (per, length), 1)
    bias = jnp.zeros((per, length), F32)
    rate = jnp.zeros((per, length), F32)
    for h in range(per):
        bias = jnp.where(head_at == h, bias_ref[h], bias)
        rate = jnp.where(head_at == h, alog_ref[h], rate)
    pre = raw + bias
    step = jnp.maximum(pre, 0.0) + jnp.log1p(jnp.exp(-jnp.abs(pre)))
    squash = jax.nn.sigmoid(pre)
    decay = -jnp.exp(rate) * step
    cum = decay
    reach = 1
    while reach < length:
        cum = cum + jnp.where(token_at >= reach, pltpu.roll(cum, reach, 1), 0.0)
        reach *= 2
    for d in range(row):
        pair = slice(2 * d, 2 * d + 2)
        sdt[d] = jnp.concatenate([step[pair], cum[pair], squash[pair], decay[pair]], axis=0)
    keep(sdt.at[r], rdt.at[r], dt_recv.at[r])

    def send_dt(i):
        to = lax.rem(r + i, row)
        send(sdt.at[to], rdt.at[r], dt_send, dt_recv.at[r], at(to, z))

    loop(1, row, send_dt)
    loop(AHEAD * zs, row * zs, send_x)

    def send_c(i):
        to = lax.rem(r + i, row)
        send(rzb.at[1], rc.at[r], c_send, c_recv.at[r], at(to, z))

    loop(1, row, send_c)

    def gate(d):
        zf, of = z_ref[:, lanes_of(d)].astype(F32), og_ref[:, lanes_of(d)].astype(F32)
        s = jax.nn.sigmoid(zf)
        sg[d] = (of * (zf * s)).astype(BF16)
        slope[:, lanes_of(d)] = of * (s * (1.0 + zf * (1.0 - s)))

    gate(z * row + r)
    keep(sg.at[z * row + r], rg.at[r, mine, :], g_recv.at[r])

    def send_g(i):
        r_to, z_to = other(i)
        d = z_to * row + r_to
        gate(d)
        send(sg.at[d], rg.at[r, mine, :], g_send, g_recv.at[r], at(r_to, z_to))

    loop(1, row * zs, send_g)

    lane = lax.broadcasted_iota(jnp.int32, (1, LANES), 1)
    first = lane < HALF
    sel = [first.astype(F32), 1.0 - first.astype(F32)]
    skip = jnp.where(first, skip_ref[2 * r], skip_ref[2 * r + 1])
    at_row = lax.broadcasted_iota(jnp.int32, (length, length), 0)
    at_col = lax.broadcasted_iota(jnp.int32, (length, length), 1)
    causal = at_row >= at_col
    before = (at_row < at_col).astype(F32)
    sel_at = lax.broadcasted_iota(jnp.int32, (16, LANES), 0)
    sel_lane = lax.broadcasted_iota(jnp.int32, (16, LANES), 1)
    pick = jnp.where(sel_at == lax.div(sel_lane, HALF), 1.0, 0.0)
    pick16 = pick.astype(BF16)

    def chunk(k):
        return lax.rem(r + row - k, row)

    def last_decay(c):
        rows = rdt[c]
        return jnp.exp(jnp.where(first, rows[2:3, length - 1 :], rows[3:4, length - 1 :]))

    def with_keep(total, keep_all):
        high = keep_all.astype(BF16).astype(F32)
        mid = (keep_all - high).astype(BF16).astype(F32)
        low = keep_all - high - mid
        tail = jnp.where(sel_at == 0, high, jnp.where(sel_at == 1, mid, low))
        return jnp.concatenate([total.astype(BF16), tail.astype(BF16)], axis=0)

    def states(k):
        c = chunk(k)
        bytes_wait(rdt.at[c], dt_recv.at[c])
        rows = rdt[c]
        across = jnp.transpose(rows)
        cols[c] = across
        up = jnp.where(first, across[:, 2:3], across[:, 3:4])
        end = jnp.where(first, rows[2:3, length - 1 :], rows[3:4, length - 1 :])
        size = jnp.where(first, across[:, 0:1], across[:, 1:2])
        w = jnp.exp(end - up) * size
        ecol[c] = jnp.exp(up)
        wcol[c] = w
        bytes_wait(rb.at[c], b_recv.at[c])
        bytes_wait(rx.at[c], x_recv.at[c])
        grown = (w * rx[c].astype(F32)).astype(BF16)
        wx[c] = grown
        st_s[c] = mm(rb[c], grown, 0, 0)

    loop(0, row, states)
    state = jnp.zeros((STATE, LANES), F32)
    keep_all = jnp.ones((1, LANES), F32)
    for c in range(row):
        fade = last_decay(c)
        keep_all = keep_all * fade
        state = fade * state + st_s[c]
    ssend[...] = with_keep(state, keep_all)

    def send_s(i):
        @pl.when(y + i < slabs)
        def _():
            send(ssend, srecv.at[y], s_send, s_recv.at[y], ((y + i) * row + r, z))

    loop(1, slabs, send_s)

    def scored(k):
        c = chunk(k)
        bytes_wait(rc.at[c], c_recv.at[c])
        xf = rx[c].astype(F32)
        across = cols[c]
        aff = mm(rc[c], rb[c], 1, 1)
        affs[c] = aff
        y_sum = skip * xf
        for j in range(2):
            fall = across[:, 2 + j : 3 + j] - rdt[c, 2 + j : 3 + j, :]
            e = jnp.where(causal, jnp.exp(fall), 0.0)
            decs[c, j] = e
            score = (e * aff * rdt[c, j : j + 1, :]).astype(BF16)
            scores[c, j] = score
            y_sum = y_sum + mm(score, (xf * sel[j]).astype(BF16), 1, 0)
        y_in[c] = y_sum

    loop(0, row, scored)

    def cotangents(k):
        c = chunk(k)
        bytes_wait(rg.at[c], g_recv.at[c])
        faded = (ecol[c] * rg[c].astype(F32)).astype(BF16)
        eg[c] = faded
        st_a[c] = mm(rc[c], faded, 0, 0)

    loop(0, row, cotangents)
    back = jnp.zeros((STATE, LANES), F32)
    for c in reversed(range(row)):
        back = last_decay(c) * back + st_a[c]
    asend[...] = with_keep(back, keep_all)

    def send_a(i):
        @pl.when(y >= i)
        def _():
            send(asend, arecv.at[y], a_send, a_recv.at[y], ((y - i) * row + r, z))

    loop(1, slabs, send_a)

    state = jnp.zeros((STATE, LANES), F32)
    srecv[y] = ssend[...]
    for i in reversed(range(1, slabs)):
        source = lax.rem(y + slabs - i, slabs)

        @pl.when(y >= i)
        def _():
            bytes_wait(srecv.at[source], s_recv.at[source])

        ends = srecv[source, STATE : STATE + 16].astype(F32)
        fade = ends[0:1] + ends[1:2] + ends[2:3]
        state = jnp.where(y >= i, fade * state + srecv[source, 0:STATE].astype(F32), state)
    for c in range(row):
        hb[c] = state.astype(BF16)
        here = st_s[c]
        st_s[c] = state
        state = last_decay(c) * state + here

    there = lanes_of(z * row + r)

    def leave(buffer, k, c, landing, send_sem, recv_sem):
        @pl.when(k == 0)
        def _():
            keep(buffer.at[c, mine, :], landing.at[:, there], recv_sem)

        @pl.when(k > 0)
        def _():
            send(buffer.at[c, mine, :], landing.at[:, there], send_sem, recv_sem, at(c, z))

        def one(i):
            to = lax.rem(z + i, zs)
            part = buffer.at[c, tokens_of(to), :]
            send(part, landing.at[:, there], send_sem, recv_sem, at(c, to))

        loop(1, zs, one)

    def finish_y(k):
        c = lax.rem(r + k, row)
        yi = ecol[c] * mm(rc[c], hb[c], 1, 0)
        sy[c] = (y_in[c] + yi).astype(BF16)
        leave(sy, k, c, ry, y_send, y_recv)
        rho[c] = mm(pick16, (rg[c].astype(F32) * yi).astype(BF16), 1, 1)[0:8]

    loop(0, row, finish_y)

    skipsum[...] = jnp.zeros_like(skipsum)

    def pulled(k):
        c = lax.rem(r + k, row)
        xs, gs, bs, cs = rx[c], rg[c], rb[c], rc[c]
        xf, gf = xs.astype(F32), gs.astype(F32)
        aff = affs[c]
        dx_sum = skip * gf
        pulls = jnp.zeros((length, length), F32)
        for j in range(2):
            g_j = (gf * sel[j]).astype(BF16)
            size = rdt[c, j : j + 1, :]
            k1 = decs[c, j] * mm(g_j, xs, 1, 1)
            k0 = k1 * aff
            ds0[c, j : j + 1, :] = jnp.sum(k0, axis=0, keepdims=True)
            crossing = mm((k0 * size).astype(BF16), before.astype(BF16), 1, 0)
            dla0[c, j : j + 1, :] = jnp.sum(
                jnp.where(causal, crossing, 0.0), axis=0, keepdims=True
            )
            pulls = pulls + k1 * size
            dx_sum = dx_sum + mm(scores[c, j], g_j, 0, 0)
        pulls = pulls.astype(BF16)
        dx_in[c] = dx_sum
        sdc[c] = (mm(pulls, bs, 1, 0) + mm(eg[c], hb[c], 1, 1)).astype(BF16)
        db_in[c] = mm(pulls, cs, 0, 0)
        skipsum[...] = skipsum[...] + jnp.sum(xf * gf, axis=0, keepdims=True)

        @pl.when(k == 0)
        def _():
            keep(sdc.at[c], rdc.at[r], dc_recv.at[r])

        @pl.when(k > 0)
        def _():
            send(sdc.at[c], rdc.at[r], dc_send, dc_recv.at[r], at(c, z))

    loop(0, row, pulled)

    back = jnp.zeros((STATE, LANES), F32)
    arecv[y] = asend[...]
    for i in reversed(range(1, slabs)):
        source = lax.rem(y + i, slabs)

        @pl.when(y + i < slabs)
        def _():
            bytes_wait(arecv.at[source], a_recv.at[source])

        ends = arecv[source, STATE : STATE + 16].astype(F32)
        fade = ends[0:1] + ends[1:2] + ends[2:3]
        part = arecv[source, 0:STATE].astype(F32)
        back = jnp.where(y + i < slabs, fade * back + part, back)
    for c in reversed(range(row)):
        hb[c] = back.astype(BF16)
        fade = last_decay(c)
        over = fade * jnp.sum(st_s[c] * back, axis=0, keepdims=True)
        cterm[c] = jnp.broadcast_to(
            jnp.sum(pick[0:8] * over, axis=1, keepdims=True), (8, length)
        )
        back = fade * back + st_a[c]

    def finish_x(k):
        c = lax.rem(r + k, row)
        bi = wcol[c] * mm(rb[c], hb[c], 1, 0)
        sdx[c] = (dx_in[c] + bi).astype(BF16)
        leave(sdx, k, c, rdx, dx_send, dx_recv)
        sdb[c] = (db_in[c] + mm(wx[c], hb[c], 1, 1)).astype(BF16)

        @pl.when(k == 0)
        def _():
            keep(sdb.at[c], rdb.at[r], db_recv.at[r])

        @pl.when(k > 0)
        def _():
            send(sdb.at[c], rdb.at[r], db_send, db_recv.at[r], at(c, z))

        kap[c] = mm(pick16, (rx[c].astype(F32) * bi).astype(BF16), 1, 1)[0:8]

    loop(0, row, finish_x)

    flat = (row * 8, length)
    dla = (
        dla0[...].reshape(flat)
        + mm_exact(rho[...].reshape(flat), causal.astype(F32))
        + mm_exact(kap[...].reshape(flat), before)
        + cterm[...].reshape(flat)
    )
    parts = [rdt[c] for c in range(row)]
    steps = jnp.concatenate(parts, axis=0)
    squashes = jnp.concatenate([pltpu.roll(p, 4, 0) for p in parts], axis=0)
    decays = jnp.concatenate([pltpu.roll(p, 2, 0) for p in parts], axis=0)
    which = lax.rem(lax.broadcasted_iota(jnp.int32, flat, 0), 8)
    rates = jnp.exp(jnp.where(which == 0, alog_ref[2 * r], alog_ref[2 * r + 1]))
    dsteps = ds0[...].reshape(flat) + kap[...].reshape(flat) / steps - rates * dla
    draws = jnp.where(which < 2, dsteps * squashes, 0.0)
    dlogs = jnp.where(which < 2, dla * decays, 0.0)
    sgd[...] = draws.reshape(row, 8, length)
    keep(sgd.at[r], rgd.at[r], gd_recv.at[r])

    def send_gd(i):
        to = lax.rem(r + i, row)
        send(sgd.at[to], rgd.at[r], gd_send, gd_recv.at[r], at(to, z))

    loop(1, row, send_gd)

    sum_at = lax.broadcasted_iota(jnp.int32, (8, LANES), 0)
    sum_lane = lax.broadcasted_iota(jnp.int32, (8, LANES), 1)
    sums = jnp.zeros((8, LANES), F32)
    for j in range(2):
        totals = (
            jnp.sum(jnp.where(which == j, draws, 0.0)),
            jnp.sum(jnp.where(which == j, dlogs, 0.0)),
            jnp.sum(skipsum[...] * sel[j]),
        )
        for q in range(3):
            place = (sum_at == q) & (sum_lane == 2 * r + j)
            sums = jnp.where(place, totals[q], sums)
    ssy[...] = sums
    keep(ssy, rsy.at[y], sy_recv)

    def send_sy(i):
        send(ssy, rsy.at[y], sy_send, sy_recv, (lax.rem(y + i, slabs) * row + r, z))

    loop(1, slabs, send_sy)

    loop(0, row, lambda c: bytes_wait(rdc.at[c], dc_recv.at[c]))
    total = rdc[0].astype(F32)
    for c in range(1, row):
        total = total + rdc[c].astype(F32)
    szo[1] = total.astype(BF16)
    loop(0, row, lambda c: bytes_wait(rdb.at[c], db_recv.at[c]))
    total = rdb[0].astype(F32)
    for c in range(1, row):
        total = total + rdb[c].astype(F32)
    szo[0] = total.astype(BF16)
    loop(0, row, lambda c: bytes_wait(rgd.at[c], gd_recv.at[c]))
    turn[...] = jnp.zeros_like(turn)
    turn[pl.ds(pl.multiple_of(z * per, per), per), :] = jnp.concatenate(
        [rgd[c][0:2] for c in range(row)], axis=0
    )
    szo[2, :, 0:heads] = jnp.transpose(turn[...]).astype(BF16)
    keep(szo.at[:, mine, :], rzo.at[z], zo_recv)

    def send_zo(i):
        to = lax.rem(z + i, zs)
        send(szo.at[:, tokens_of(to), :], rzo.at[z], zo_send, zo_recv, at(r, to))

    loop(1, zs, send_zo)

    bytes_wait(rsy, sy_recv)
    total = rsy[0]
    for i in range(1, slabs):
        total = total + rsy[i]
    ssr[...] = total
    keep(ssr, rsr.at[r], sr_recv)

    def send_sr(i):
        send(ssr, rsr.at[r], sr_send, sr_recv, at(lax.rem(r + i, row), z))

    loop(1, row, send_sr)

    bytes_wait(ry, y_recv)

    def gate_back(d):
        inner_ref[1, :, lanes_of(d)] = (
            slope[:, lanes_of(d)] * ry[:, lanes_of(d)].astype(F32)
        ).astype(BF16)

    loop(0, row * zs, gate_back)
    bytes_wait(rdx, dx_recv)
    inner_ref[0] = rdx[...]

    bytes_wait(rzo, zo_recv)
    total = jnp.zeros((TOK, heads), F32)
    for k in range(zs):
        outer_ref[0, :, k * STATE : (k + 1) * STATE] = rzo[k, 0]
        outer_ref[1, :, k * STATE : (k + 1) * STATE] = rzo[k, 1]
        total = total + rzo[k, 2, :, 0:heads].astype(F32)
    gdt_ref[...] = total.astype(BF16)
    bytes_wait(rsr, sr_recv)
    total = rsr[0]
    for i in range(1, row):
        total = total + rsr[i]
    sums_ref[...] = total

    @pl.when(y < slabs - 1)
    def _():
        loop(0, slabs - 1 - y, lambda i: bytes_wait(ssend, s_send))

    @pl.when(y > 0)
    def _():
        loop(0, y, lambda i: bytes_wait(asend, a_send))

    blocks = sg.at[pl.ds(0, row * zs - 1)]
    for sem in (x_send, g_send, y_send, dx_send):
        bytes_wait(blocks, sem)
    others = pl.ds(0, row - 1)
    bytes_wait(sbc.at[pl.ds(0, zs - 1)], zb_send)
    bytes_wait(rb.at[others], b_send)
    bytes_wait(rc.at[others], c_send)
    bytes_wait(sdt.at[others], dt_send)
    bytes_wait(rdb.at[others], db_send)
    bytes_wait(rdc.at[others], dc_send)
    bytes_wait(sgd.at[others], gd_send)
    bytes_wait(rzo.at[pl.ds(0, zs - 1)], zo_send)
    bytes_wait(rsy.at[pl.ds(0, slabs - 1)], sy_send)
    bytes_wait(rsr.at[others], sr_send)


def unpack(
    inner_hbm, outer_hbm, dt_hbm, sums_ref,
    gx_ref, gz_ref, gb_ref, gc_ref, gdt_ref, bias_ref, alog_ref, skip_ref,
    inner, outer, dts, come, go,
):
    moves = (
        (inner_hbm.at[0], inner.at[0], gx_ref),
        (inner_hbm.at[1], inner.at[1], gz_ref),
        (outer_hbm.at[0], outer.at[0], gb_ref),
        (outer_hbm.at[1], outer.at[1], gc_ref),
        (dt_hbm, dts, gdt_ref),
    )
    came = [pltpu.make_async_copy(a, b, come.at[i]) for i, (a, b, _) in enumerate(moves)]
    gone = [pltpu.make_async_copy(b, c, go.at[i]) for i, (_, b, c) in enumerate(moves)]
    for copy in came:
        copy.start()
    for q, ref in enumerate((bias_ref, alog_ref, skip_ref)):
        ref[...] = sums_ref[q, 0 : ref.shape[0]]
    for first, second in zip(came, gone):
        first.wait()
        second.start()
    for copy in gone:
        copy.wait()


def shards(row, x_proj, z_gate, out_grad, b_proj, c_proj, dt_raw, dt_bias, a_log, d_skip):
    zs = lax.axis_size("head")
    slabs = lax.axis_size("seq") // row
    heads = 2 * row * zs
    length = zs * TOK
    inner = heads * HALF

    def vmem(*shape, dtype=BF16):
        return pltpu.VMEM(shape, dtype)

    square = (row, length, LANES)
    states = (row, STATE, LANES)
    per = 2 * row
    scratch = [
        vmem(TOK, inner),
        vmem(TOK, inner),
        vmem(TOK, inner),
        vmem(TOK, zs * STATE),
        vmem(TOK, zs * STATE),
        vmem(TOK, heads),
        pltpu.SMEM((per,), F32),
        pltpu.SMEM((per,), F32),
        pltpu.SMEM((per,), F32),
        vmem(row * zs, TOK, LANES),
        vmem(*square),
        vmem(*square),
        vmem(zs, 3, TOK, STATE),
        vmem(3, length, STATE),
        vmem(*square),
        vmem(*square),
        vmem(row, 8, length, dtype=F32),
        vmem(row, 8, length, dtype=F32),
        vmem(STATE + 16, LANES),
        vmem(STATE + 16, LANES),
        vmem(slabs, STATE + 16, LANES),
        vmem(slabs, STATE + 16, LANES),
        vmem(*square),
        vmem(*square),
        vmem(TOK, inner),
        vmem(TOK, inner),
        vmem(*square),
        vmem(*square),
        vmem(*square),
        vmem(*square),
        vmem(row, 8, length, dtype=F32),
        vmem(row, 8, length, dtype=F32),
        vmem(3, length, STATE),
        vmem(zs, 3, TOK, STATE),
        vmem(8, LANES, dtype=F32),
        vmem(slabs, 8, LANES, dtype=F32),
        vmem(8, LANES, dtype=F32),
        vmem(row, 8, LANES, dtype=F32),
        vmem(TOK, inner, dtype=F32),
        vmem(heads, length, dtype=F32),
        vmem(row, length, 8, dtype=F32),
        vmem(*square, dtype=F32),
        vmem(*square, dtype=F32),
        vmem(*square),
        vmem(*square),
        vmem(*states, dtype=F32),
        vmem(*states, dtype=F32),
        vmem(*states),
        vmem(row, length, length, dtype=F32),
        vmem(row, 2, length, length, dtype=F32),
        vmem(row, 2, length, length),
        vmem(*square, dtype=F32),
        vmem(*square, dtype=F32),
        vmem(*square, dtype=F32),
        vmem(row, 8, length, dtype=F32),
        vmem(row, 8, length, dtype=F32),
        vmem(row, 8, length, dtype=F32),
        vmem(row, 8, length, dtype=F32),
        vmem(row, 8, length, dtype=F32),
        vmem(1, LANES, dtype=F32),
    ]
    one, many = pltpu.SemaphoreType.DMA, lambda n: pltpu.SemaphoreType.DMA((n,))
    semaphores = [
        one, one,
        one, many(row),
        one, many(row),
        one, many(row),
        one, many(row),
        one, many(row),
        one, many(slabs),
        one, many(slabs),
        one, one,
        one, one,
        one, many(row),
        one, many(row),
        one, many(row),
        one, one,
        one, one,
        one, one,
        many(9),
    ]
    in_vmem = pl.BlockSpec(memory_space=pltpu.VMEM)
    in_hbm = pl.BlockSpec(memory_space=pltpu.HBM)
    like = jax.ShapeDtypeStruct
    results = pl.pallas_call(
        functools.partial(kernel, (slabs, row, zs, heads)),
        out_shape=[
            like((2, TOK, inner), BF16),
            like((2, TOK, zs * STATE), BF16),
            like((TOK, heads), BF16),
            like((8, LANES), F32),
        ],
        in_specs=[in_hbm] * 9,
        out_specs=[in_vmem] * 4,
        scratch_shapes=scratch + semaphores,
        compiler_params=pltpu.CompilerParams(
            collective_id=0, has_side_effects=True, vmem_limit_bytes=62 * 2**20
        ),
        name="scan_backward",
    )(x_proj, z_gate, out_grad, b_proj, c_proj, dt_raw, dt_bias, a_log, d_skip)
    anywhere = pl.BlockSpec(memory_space=pl.ANY)
    return pl.pallas_call(
        unpack,
        out_shape=[
            like((TOK, inner), BF16),
            like((TOK, inner), BF16),
            like((TOK, zs * STATE), BF16),
            like((TOK, zs * STATE), BF16),
            like((TOK, heads), BF16),
            like((per,), F32),
            like((per,), F32),
            like((per,), F32),
        ],
        in_specs=[anywhere] * 3 + [in_vmem],
        out_specs=[anywhere] * 5 + [in_vmem] * 3,
        scratch_shapes=[
            vmem(2, TOK, inner),
            vmem(2, TOK, zs * STATE),
            vmem(TOK, heads),
            many(5),
            many(5),
        ],
        compiler_params=pltpu.CompilerParams(vmem_limit_bytes=62 * 2**20),
        name="unpack",
    )(*results)


def solution(mesh, row=ROW):
    tokens = P(("seq", "head"), None)
    return jax.shard_map(
        functools.partial(shards, row),
        mesh=mesh,
        in_specs=(tokens,) * 6 + (P("head"),) * 3,
        out_specs=(tokens,) * 5 + (P("head"),) * 3,
        check_vma=False,
    )
```

```python
import functools

import jax
import jax.numpy as jnp
from jax import lax
from jax.experimental import pallas as pl
from jax.experimental.pallas import tpu as pltpu
from jax.sharding import PartitionSpec as P

ROW = 8
TOK = 16
WIDE = 2
FIRST = 2
STATE = 128
LANES = 128
HALF = 64
AHEAD = 8

F32 = jnp.float32
BF16 = jnp.bfloat16
MESH = pl.DeviceIdType.MESH


def mm(a, b, ca, cb):
    return lax.dot_general(a, b, (((ca,), (cb,)), ((), ())), preferred_element_type=F32)


def mm_exact(a, b):
    return lax.dot_general(
        a,
        b,
        (((1,), (0,)), ((), ())),
        precision=lax.Precision.HIGHEST,
        preferred_element_type=F32,
    )


def loop(low, high, body):
    def step(i, carry):
        body(i)
        return carry

    lax.fori_loop(low, high, step, 0)


def pairs(count, body, after=None):
    def step(k):
        for i in range(WIDE):
            body(k * WIDE + i)
        if after is not None:
            for i in range(WIDE):
                after(k * WIDE + i)

    loop(0, count // WIDE, step)


def bytes_wait(ref, sem):
    pltpu.make_async_copy(ref, ref, sem).wait()


def kernel(
    sizes,
    x_hbm, z_hbm, og_hbm, b_hbm, c_hbm, dt_hbm, bias_hbm, alog_hbm, skip_hbm,
    inner_ref, outer_ref, gdt_ref, sums_ref,
    x_ref, z_ref, og_ref, b_ref, c_ref, dt_ref, bias_ref, alog_ref, skip_ref,
    sx, sg, rx, rg, sbc, rzb, scz, rcz, rb, rc, sdt, rdt, ssend, asend, srecv, arecv, skept, rkept, fades, sy, sdx, ry, rdx,
    sdb, sdc, rdb, rdc, sgd, rgd, szo, rzo, szc, rzc, ssy, rsy, ssr, rsr,
    slope, turn, cols, ecol, wcol, eg, wx, st_s, st_a, hb, affs, decs, scores,
    y_in, dx_in, db_in, ds0, dla0, rho, kap, cterm, skipsum,
    zb_send, zb_recv, zc_send, zc_recv, x_send, x_recv, g_send, g_recv, b_send, b_recv, c_send, c_recv,
    dt_send, dt_recv, s_send, s_recv, a_send, a_recv, k_send, k_recv, y_send, y_recv, dx_send, dx_recv,
    db_send, db_recv, dc_send, dc_recv, gd_send, gd_recv, zo_send, zo_recv, oc_send, oc_recv,
    sy_send, sy_recv, sr_send, sr_recv, load,
):
    slabs, row, zs, heads = sizes
    length = zs * TOK
    per = 2 * row
    seq, z = lax.axis_index("seq"), lax.axis_index("head")
    y, r = lax.div(seq, row), lax.rem(seq, row)
    mine = pl.ds(pl.multiple_of(z * TOK, TOK), TOK)

    def at(row_to, z_to):
        return (y * row + row_to, z_to)

    def other(i):
        return lax.rem(r + lax.div(i, zs), row), lax.rem(z + lax.rem(i, zs), zs)

    def lanes_of(d):
        return pl.ds(pl.multiple_of(d * LANES, LANES), LANES)

    def tokens_of(k):
        return pl.ds(pl.multiple_of(k * TOK, TOK), TOK)

    def send(src, dst, send_sem, recv_sem, device):
        pltpu.make_async_remote_copy(
            src_ref=src,
            dst_ref=dst,
            send_sem=send_sem,
            recv_sem=recv_sem,
            device_id=device,
            device_id_type=MESH,
        ).start()

    def keep(src, dst, recv_sem):
        pltpu.make_async_copy(src, dst, recv_sem).start()

    barrier = pltpu.get_barrier_semaphore()

    def greet(i):
        pl.semaphore_signal(barrier, inc=1, device_id=at(*other(i)), device_id_type=MESH)

    def greet_slab(i):
        there = (lax.rem(y + i, slabs) * row + r, z)
        pl.semaphore_signal(barrier, inc=1, device_id=there, device_id_type=MESH)

    loop(1, row * zs, greet)
    loop(1, slabs, greet_slab)

    loads = [
        pltpu.make_async_copy(there, here, load.at[i])
        for i, (there, here) in enumerate(
            (
                (b_hbm, b_ref),
                (c_hbm, c_ref),
                (dt_hbm, dt_ref),
                (x_hbm, x_ref),
                (z_hbm, z_ref),
                (og_hbm, og_ref),
                (bias_hbm, bias_ref),
                (alog_hbm, alog_ref),
                (skip_hbm, skip_ref),
            )
        )
    ]
    for copy in loads:
        copy.start()

    for copy in loads[:3]:
        copy.wait()
    for k in range(zs):
        sbc[k, 0] = b_ref[:, k * STATE : (k + 1) * STATE]
        sbc[k, 1, :, 0:heads] = dt_ref[...]
        scz[k] = c_ref[:, k * STATE : (k + 1) * STATE]
    loads[3].wait()
    for d in range(row * zs):
        sx[d] = x_ref[:, d * LANES : (d + 1) * LANES]
    pl.semaphore_wait(barrier, row * zs - 1 + slabs - 1)

    keep(sbc.at[z], rzb.at[:, mine, :], zb_recv)

    def send_zb(i):
        to = lax.rem(z + i, zs)
        send(sbc.at[to], rzb.at[:, mine, :], zb_send, zb_recv, at(r, to))

    loop(1, zs, send_zb)

    keep(sx.at[z * row + r], rx.at[r, mine, :], x_recv.at[r])

    def send_x(i):
        r_to, z_to = other(i)
        send(
            sx.at[z_to * row + r_to],
            rx.at[r, mine, :],
            x_send,
            x_recv.at[r],
            at(r_to, z_to),
        )

    loop(1, AHEAD * zs, send_x)

    keep(scz.at[z], rcz.at[mine, :], zc_recv)

    def send_zc(i):
        to = lax.rem(z + i, zs)
        send(scz.at[to], rcz.at[mine, :], zc_send, zc_recv, at(r, to))

    loop(1, zs, send_zc)

    bytes_wait(rzb, zb_recv)
    keep(rzb.at[0], rb.at[r], b_recv.at[r])

    def send_b(i):
        to = lax.rem(r + i, row)
        send(rzb.at[0], rb.at[r], b_send, b_recv.at[r], at(to, z))

    loop(1, row, send_b)

    loop(AHEAD * zs, row * zs, send_x)

    for copy in loads[4:]:
        copy.wait()
    turn[...] = jnp.transpose(rzb[1].astype(F32)[:, 0:heads])
    raw = turn[pl.ds(pl.multiple_of(z * per, per), per), :]
    head_at = lax.broadcasted_iota(jnp.int32, (per, length), 0)
    token_at = lax.broadcasted_iota(jnp.int32, (per, length), 1)
    bias = jnp.zeros((per, length), F32)
    rate = jnp.zeros((per, length), F32)
    for h in range(per):
        bias = jnp.where(head_at == h, bias_ref[h], bias)
        rate = jnp.where(head_at == h, alog_ref[h], rate)
    pre = raw + bias
    step = jnp.maximum(pre, 0.0) + jnp.log1p(jnp.exp(-jnp.abs(pre)))
    squash = jax.nn.sigmoid(pre)
    decay = -jnp.exp(rate) * step
    cum = decay
    reach = 1
    while reach < length:
        cum = cum + jnp.where(token_at >= reach, pltpu.roll(cum, reach, 1), 0.0)
        reach *= 2
    for d in range(row):
        pair = slice(2 * d, 2 * d + 2)
        sdt[d] = jnp.concatenate([step[pair], cum[pair], squash[pair], decay[pair]], axis=0)
    keep(sdt.at[r], rdt.at[r], dt_recv.at[r])

    def send_dt(i):
        to = lax.rem(r + i, row)
        send(sdt.at[to], rdt.at[r], dt_send, dt_recv.at[r], at(to, z))

    loop(1, row, send_dt)

    def gate(k):
        for i in range(row):
            d = k * row + i
            zf, of = z_ref[:, lanes_of(d)].astype(F32), og_ref[:, lanes_of(d)].astype(F32)
            s = jax.nn.sigmoid(zf)
            sg[d] = (of * (zf * s)).astype(BF16)
            slope[d] = of * (s * (1.0 + zf * (1.0 - s)))

    loop(0, zs, gate)
    keep(sg.at[z * row + r], rg.at[r, mine, :], g_recv.at[r])

    def send_g(i):
        r_to, z_to = other(i)
        send(sg.at[z_to * row + r_to], rg.at[r, mine, :], g_send, g_recv.at[r], at(r_to, z_to))

    loop(1, row * zs, send_g)

    bytes_wait(rcz, zc_recv)
    keep(rcz, rc.at[r], c_recv.at[r])

    def send_c(i):
        to = lax.rem(r + i, row)
        send(rcz, rc.at[r], c_send, c_recv.at[r], at(to, z))

    loop(1, row, send_c)

    lane = lax.broadcasted_iota(jnp.int32, (1, LANES), 1)
    first = lane < HALF
    sel = [first.astype(F32), 1.0 - first.astype(F32)]
    skip = jnp.where(first, skip_ref[2 * r], skip_ref[2 * r + 1])
    at_row = lax.broadcasted_iota(jnp.int32, (length, length), 0)
    at_col = lax.broadcasted_iota(jnp.int32, (length, length), 1)
    causal = at_row >= at_col
    before = (at_row < at_col).astype(F32)
    sel_at = lax.broadcasted_iota(jnp.int32, (16, LANES), 0)
    sel_lane = lax.broadcasted_iota(jnp.int32, (16, LANES), 1)
    pick = jnp.where(sel_at == lax.div(sel_lane, HALF), 1.0, 0.0)
    pick16 = pick.astype(BF16)

    def chunk(k):
        return lax.rem(r + row - k, row)

    def last_decay(c):
        return fades[c, 0:1]

    def decays_of(k):
        c = chunk(k)
        rows = rdt[c]
        across = jnp.transpose(rows)
        cols[c] = across
        up = jnp.where(first, across[:, 2:3], across[:, 3:4])
        end = jnp.where(first, rows[2:3, length - 1 :], rows[3:4, length - 1 :])
        size = jnp.where(first, across[:, 0:1], across[:, 1:2])
        ecol[c] = jnp.exp(up)
        wcol[c] = jnp.exp(end - up) * size
        fades[c] = jnp.broadcast_to(jnp.exp(end), (8, LANES))

    loop(0, row, lambda c: bytes_wait(rdt.at[c], dt_recv.at[c]))
    pairs(row, decays_of)
    kept = fades[0]
    for c in range(1, row):
        kept = kept * fades[c]
    skept[...] = kept

    def send_kept(i):
        there = (lax.rem(y + i, slabs) * row + r, z)
        send(skept, rkept.at[y], k_send, k_recv.at[y], there)

    loop(1, slabs, send_kept)

    def states(k):
        c = chunk(k)
        bytes_wait(rb.at[c], b_recv.at[c])
        bytes_wait(rx.at[c], x_recv.at[c])
        grown = (wcol[c] * rx[c].astype(F32)).astype(BF16)
        wx[c] = grown
        st_s[c] = mm(rb[c], grown, 0, 0)

    loop(0, row, states)
    state = jnp.zeros((STATE, LANES), F32)
    for c in range(row):
        state = last_decay(c) * state + st_s[c]
    ssend[...] = state.astype(BF16)

    def send_s(i):
        @pl.when(y + i < slabs)
        def _():
            send(ssend, srecv.at[y], s_send, s_recv.at[y], ((y + i) * row + r, z))

    loop(1, slabs, send_s)

    def scored(k):
        c = chunk(k)
        xf = rx[c].astype(F32)
        across = cols[c]
        aff = mm(rc[c], rb[c], 1, 1)
        affs[c] = aff
        y_sum = skip * xf
        for j in range(2):
            fall = across[:, 2 + j : 3 + j] - rdt[c, 2 + j : 3 + j, :]
            e = jnp.where(causal, jnp.exp(fall), 0.0)
            decs[c, j] = e
            score = (e * aff * rdt[c, j : j + 1, :]).astype(BF16)
            scores[c, j] = score
            y_sum = y_sum + mm(score, (xf * sel[j]).astype(BF16), 1, 0)
        y_in[c] = y_sum

    loop(0, row, lambda c: bytes_wait(rc.at[c], c_recv.at[c]))
    pairs(row, scored)

    def cotangents(k):
        c = chunk(k)
        bytes_wait(rg.at[c], g_recv.at[c])
        faded = (ecol[c] * rg[c].astype(F32)).astype(BF16)
        eg[c] = faded
        st_a[c] = mm(rc[c], faded, 0, 0)

    loop(0, row, cotangents)
    back = jnp.zeros((STATE, LANES), F32)
    for c in reversed(range(row)):
        back = last_decay(c) * back + st_a[c]
    asend[...] = back.astype(BF16)

    def send_a(i):
        @pl.when(y >= i)
        def _():
            send(asend, arecv.at[y], a_send, a_recv.at[y], ((y - i) * row + r, z))

    loop(1, slabs, send_a)

    def await_kept(source):
        bytes_wait(rkept.at[source], k_recv.at[source])

    loop(1, slabs, lambda i: await_kept(lax.rem(y + i, slabs)))
    state = jnp.zeros((STATE, LANES), F32)
    for i in reversed(range(1, slabs)):
        source = lax.rem(y + slabs - i, slabs)

        @pl.when(y >= i)
        def _():
            bytes_wait(srecv.at[source], s_recv.at[source])

        fade = rkept[source, 0:1]
        state = jnp.where(y >= i, fade * state + srecv[source].astype(F32), state)
    for c in range(row):
        hb[c] = state.astype(BF16)
        here = st_s[c]
        st_s[c] = state
        state = last_decay(c) * state + here

    there = z * row + r

    def leave(buffer, k, c, landing, send_sem, recv_sem):
        @pl.when(k == 0)
        def _():
            keep(buffer.at[c, mine, :], landing.at[there], recv_sem)

        @pl.when(k > 0)
        def _():
            send(buffer.at[c, mine, :], landing.at[there], send_sem, recv_sem, at(c, z))

        def one(i):
            to = lax.rem(z + i, zs)
            part = buffer.at[c, tokens_of(to), :]
            send(part, landing.at[there], send_sem, recv_sem, at(c, to))

        loop(1, zs, one)

    def finish_y(k):
        c = lax.rem(r + k, row)
        yi = ecol[c] * mm(rc[c], hb[c], 1, 0)
        sy[c] = (y_in[c] + yi).astype(BF16)
        rho[c] = mm(pick16, (rg[c].astype(F32) * yi).astype(BF16), 1, 1)[0:8]

    def leave_y(k):
        leave(sy, k, lax.rem(r + k, row), ry, y_send, y_recv)

    pairs(row, finish_y, leave_y)

    def pulled(k):
        c = lax.rem(r + k, row)
        xs, gs, bs, cs = rx[c], rg[c], rb[c], rc[c]
        xf, gf = xs.astype(F32), gs.astype(F32)
        aff = affs[c]
        dx_sum = skip * gf
        pulls = jnp.zeros((length, length), F32)
        for j in range(2):
            g_j = (gf * sel[j]).astype(BF16)
            size = rdt[c, j : j + 1, :]
            k1 = decs[c, j] * mm(g_j, xs, 1, 1)
            k0 = k1 * aff
            ds0[c, j : j + 1, :] = jnp.sum(k0, axis=0, keepdims=True)
            crossing = mm((k0 * size).astype(BF16), before.astype(BF16), 1, 0)
            dla0[c, j : j + 1, :] = jnp.sum(
                jnp.where(causal, crossing, 0.0), axis=0, keepdims=True
            )
            pulls = pulls + k1 * size
            dx_sum = dx_sum + mm(scores[c, j], g_j, 0, 0)
        pulls = pulls.astype(BF16)
        dx_in[c] = dx_sum
        sdc[c] = (mm(pulls, bs, 1, 0) + mm(eg[c], hb[c], 1, 1)).astype(BF16)
        db_in[c] = mm(pulls, cs, 0, 0)
        skipsum[pl.ds(c, 1), :] = jnp.sum(xf * gf, axis=0, keepdims=True)

    def leave_c(k):
        c = lax.rem(r + k, row)

        @pl.when(k == 0)
        def _():
            keep(sdc.at[c], rdc.at[r], dc_recv.at[r])

        @pl.when(k > 0)
        def _():
            send(sdc.at[c], rdc.at[r], dc_send, dc_recv.at[r], at(c, z))

    pairs(row, pulled, leave_c)

    back = jnp.zeros((STATE, LANES), F32)
    for i in reversed(range(1, slabs)):
        source = lax.rem(y + i, slabs)

        @pl.when(y + i < slabs)
        def _():
            bytes_wait(arecv.at[source], a_recv.at[source])

        fade, part = rkept[source, 0:1], arecv[source].astype(F32)
        back = jnp.where(y + i < slabs, fade * back + part, back)
    for c in reversed(range(row)):
        hb[c] = back.astype(BF16)
        fade = last_decay(c)
        over = fade * jnp.sum(st_s[c] * back, axis=0, keepdims=True)
        cterm[c] = jnp.broadcast_to(
            jnp.sum(pick[0:8] * over, axis=1, keepdims=True), (8, length)
        )
        back = fade * back + st_a[c]

    def finish_x(k):
        c = lax.rem(r + k, row)
        bi = wcol[c] * mm(rb[c], hb[c], 1, 0)
        sdx[c] = (dx_in[c] + bi).astype(BF16)
        sdb[c] = (db_in[c] + mm(wx[c], hb[c], 1, 1)).astype(BF16)
        kap[c] = mm(pick16, (rx[c].astype(F32) * bi).astype(BF16), 1, 1)[0:8]

    def leave_x(k):
        leave(sdx, k, lax.rem(r + k, row), rdx, dx_send, dx_recv)

    def leave_b(k):
        c = lax.rem(r + k, row)

        @pl.when(k == 0)
        def _():
            keep(sdb.at[c], rdb.at[r], db_recv.at[r])

        @pl.when(k > 0)
        def _():
            send(sdb.at[c], rdb.at[r], db_send, db_recv.at[r], at(c, z))

        @pl.when(k < FIRST)
        def _():
            leave_x(k)

    pairs(row, finish_x, leave_b)

    loop(0, row, lambda c: bytes_wait(rdc.at[c], dc_recv.at[c]))
    total = rdc[0].astype(F32)
    for c in range(1, row):
        total = total + rdc[c].astype(F32)
    szc[...] = total.astype(BF16)
    keep(szc.at[mine, :], rzc.at[z], oc_recv)

    def send_oc(i):
        to = lax.rem(z + i, zs)
        send(szc.at[tokens_of(to), :], rzc.at[z], oc_send, oc_recv, at(r, to))

    loop(1, zs, send_oc)

    flat = (row * 8, length)
    dla = (
        dla0[...].reshape(flat)
        + mm_exact(rho[...].reshape(flat), causal.astype(F32))
        + mm_exact(kap[...].reshape(flat), before)
        + cterm[...].reshape(flat)
    )
    parts = [rdt[c] for c in range(row)]
    steps = jnp.concatenate(parts, axis=0)
    squashes = jnp.concatenate([pltpu.roll(p, 4, 0) for p in parts], axis=0)
    decays = jnp.concatenate([pltpu.roll(p, 2, 0) for p in parts], axis=0)
    which = lax.rem(lax.broadcasted_iota(jnp.int32, flat, 0), 8)
    rates = jnp.exp(jnp.where(which == 0, alog_ref[2 * r], alog_ref[2 * r + 1]))
    dsteps = ds0[...].reshape(flat) + kap[...].reshape(flat) / steps - rates * dla
    draws = jnp.where(which < 2, dsteps * squashes, 0.0)
    dlogs = jnp.where(which < 2, dla * decays, 0.0)
    sgd[...] = draws.reshape(row, 8, length)
    keep(sgd.at[r], rgd.at[r], gd_recv.at[r])

    def send_gd(i):
        to = lax.rem(r + i, row)
        send(sgd.at[to], rgd.at[r], gd_send, gd_recv.at[r], at(to, z))

    loop(1, row, send_gd)

    sum_at = lax.broadcasted_iota(jnp.int32, (8, LANES), 0)
    sum_lane = lax.broadcasted_iota(jnp.int32, (8, LANES), 1)
    sums = jnp.zeros((8, LANES), F32)
    for j in range(2):
        totals = (
            jnp.sum(jnp.where(which == j, draws, 0.0)),
            jnp.sum(jnp.where(which == j, dlogs, 0.0)),
            jnp.sum(skipsum[...] * sel[j]),
        )
        for q in range(3):
            place = (sum_at == q) & (sum_lane == 2 * r + j)
            sums = jnp.where(place, totals[q], sums)
    ssy[...] = sums
    keep(ssy, rsy.at[y], sy_recv)

    def send_sy(i):
        send(ssy, rsy.at[y], sy_send, sy_recv, (lax.rem(y + i, slabs) * row + r, z))

    loop(1, slabs, send_sy)
    loop(FIRST, row, leave_x)

    loop(0, row, lambda c: bytes_wait(rdb.at[c], db_recv.at[c]))
    total = rdb[0].astype(F32)
    for c in range(1, row):
        total = total + rdb[c].astype(F32)
    szo[0] = total.astype(BF16)
    loop(0, row, lambda c: bytes_wait(rgd.at[c], gd_recv.at[c]))
    turn[...] = jnp.zeros_like(turn)
    turn[pl.ds(pl.multiple_of(z * per, per), per), :] = jnp.concatenate(
        [rgd[c][0:2] for c in range(row)], axis=0
    )
    szo[1, :, 0:heads] = jnp.transpose(turn[...]).astype(BF16)
    keep(szo.at[:, mine, :], rzo.at[z], zo_recv)

    def send_zo(i):
        to = lax.rem(z + i, zs)
        send(szo.at[:, tokens_of(to), :], rzo.at[z], zo_send, zo_recv, at(r, to))

    loop(1, zs, send_zo)

    bytes_wait(rsy, sy_recv)
    total = rsy[0]
    for i in range(1, slabs):
        total = total + rsy[i]
    ssr[...] = total
    keep(ssr, rsr.at[r], sr_recv)

    def send_sr(i):
        send(ssr, rsr.at[r], sr_send, sr_recv, at(lax.rem(r + i, row), z))

    loop(1, row, send_sr)

    bytes_wait(ry, y_recv)

    def gate_back(k):
        for i in range(row):
            d = k * row + i
            inner_ref[1, :, lanes_of(d)] = (slope[d] * ry[d].astype(F32)).astype(BF16)

    loop(0, zs, gate_back)
    bytes_wait(rzc, oc_recv)
    for k in range(zs):
        outer_ref[1, :, k * STATE : (k + 1) * STATE] = rzc[k]
    bytes_wait(rdx, dx_recv)
    for d in range(row * zs):
        inner_ref[0, :, d * LANES : (d + 1) * LANES] = rdx[d]

    bytes_wait(rzo, zo_recv)
    total = jnp.zeros((TOK, heads), F32)
    for k in range(zs):
        outer_ref[0, :, k * STATE : (k + 1) * STATE] = rzo[k, 0]
        total = total + rzo[k, 1, :, 0:heads].astype(F32)
    gdt_ref[...] = total.astype(BF16)
    bytes_wait(rsr, sr_recv)
    total = rsr[0]
    for i in range(1, row):
        total = total + rsr[i]
    sums_ref[...] = total

    @pl.when(y < slabs - 1)
    def _():
        loop(0, slabs - 1 - y, lambda i: bytes_wait(ssend, s_send))

    @pl.when(y > 0)
    def _():
        loop(0, y, lambda i: bytes_wait(asend, a_send))

    blocks = sg.at[pl.ds(0, row * zs - 1)]
    for sem in (x_send, g_send, y_send, dx_send):
        bytes_wait(blocks, sem)
    others = pl.ds(0, row - 1)
    bytes_wait(sbc.at[pl.ds(0, zs - 1)], zb_send)
    bytes_wait(scz.at[pl.ds(0, zs - 1)], zc_send)
    bytes_wait(rb.at[others], b_send)
    bytes_wait(rc.at[others], c_send)
    bytes_wait(sdt.at[others], dt_send)
    bytes_wait(rdb.at[others], db_send)
    bytes_wait(rdc.at[others], dc_send)
    bytes_wait(sgd.at[others], gd_send)
    bytes_wait(rzo.at[pl.ds(0, zs - 1)], zo_send)
    bytes_wait(rzc.at[pl.ds(0, zs - 1)], oc_send)
    bytes_wait(rsy.at[pl.ds(0, slabs - 1)], sy_send)
    bytes_wait(rsr.at[others], sr_send)
    bytes_wait(rkept.at[pl.ds(0, slabs - 1)], k_send)


def unpack(
    inner_hbm, outer_hbm, dt_hbm, sums_ref,
    gx_ref, gz_ref, gb_ref, gc_ref, gdt_ref, bias_ref, alog_ref, skip_ref,
    inner, outer, dts, come, go,
):
    moves = (
        (inner_hbm.at[0], inner.at[0], gx_ref),
        (inner_hbm.at[1], inner.at[1], gz_ref),
        (outer_hbm.at[0], outer.at[0], gb_ref),
        (outer_hbm.at[1], outer.at[1], gc_ref),
        (dt_hbm, dts, gdt_ref),
    )
    came = [pltpu.make_async_copy(a, b, come.at[i]) for i, (a, b, _) in enumerate(moves)]
    gone = [pltpu.make_async_copy(b, c, go.at[i]) for i, (_, b, c) in enumerate(moves)]
    for copy in came:
        copy.start()
    for q, ref in enumerate((bias_ref, alog_ref, skip_ref)):
        ref[...] = sums_ref[q, 0 : ref.shape[0]]
    for first, second in zip(came, gone):
        first.wait()
        second.start()
    for copy in gone:
        copy.wait()


def shards(row, x_proj, z_gate, out_grad, b_proj, c_proj, dt_raw, dt_bias, a_log, d_skip):
    zs = lax.axis_size("head")
    slabs = lax.axis_size("seq") // row
    heads = 2 * row * zs
    length = zs * TOK
    inner = heads * HALF

    def vmem(*shape, dtype=BF16):
        return pltpu.VMEM(shape, dtype)

    square = (row, length, LANES)
    states = (row, STATE, LANES)
    per = 2 * row
    scratch = [
        vmem(TOK, inner),
        vmem(TOK, inner),
        vmem(TOK, inner),
        vmem(TOK, zs * STATE),
        vmem(TOK, zs * STATE),
        vmem(TOK, heads),
        pltpu.SMEM((per,), F32),
        pltpu.SMEM((per,), F32),
        pltpu.SMEM((per,), F32),
        vmem(row * zs, TOK, LANES),
        vmem(row * zs, TOK, LANES),
        vmem(*square),
        vmem(*square),
        vmem(zs, 2, TOK, STATE),
        vmem(2, length, STATE),
        vmem(zs, TOK, STATE),
        vmem(length, STATE),
        vmem(*square),
        vmem(*square),
        vmem(row, 8, length, dtype=F32),
        vmem(row, 8, length, dtype=F32),
        vmem(STATE, LANES),
        vmem(STATE, LANES),
        vmem(slabs, STATE, LANES),
        vmem(slabs, STATE, LANES),
        vmem(8, LANES, dtype=F32),
        vmem(slabs, 8, LANES, dtype=F32),
        vmem(row, 8, LANES, dtype=F32),
        vmem(*square),
        vmem(*square),
        vmem(row * zs, TOK, LANES),
        vmem(row * zs, TOK, LANES),
        vmem(*square),
        vmem(*square),
        vmem(*square),
        vmem(*square),
        vmem(row, 8, length, dtype=F32),
        vmem(row, 8, length, dtype=F32),
        vmem(2, length, STATE),
        vmem(zs, 2, TOK, STATE),
        vmem(length, STATE),
        vmem(zs, TOK, STATE),
        vmem(8, LANES, dtype=F32),
        vmem(slabs, 8, LANES, dtype=F32),
        vmem(8, LANES, dtype=F32),
        vmem(row, 8, LANES, dtype=F32),
        vmem(row * zs, TOK, LANES, dtype=F32),
        vmem(heads, length, dtype=F32),
        vmem(row, length, 8, dtype=F32),
        vmem(*square, dtype=F32),
        vmem(*square, dtype=F32),
        vmem(*square),
        vmem(*square),
        vmem(*states, dtype=F32),
        vmem(*states, dtype=F32),
        vmem(*states),
        vmem(row, length, length, dtype=F32),
        vmem(row, 2, length, length, dtype=F32),
        vmem(row, 2, length, length),
        vmem(*square, dtype=F32),
        vmem(*square, dtype=F32),
        vmem(*square, dtype=F32),
        vmem(row, 8, length, dtype=F32),
        vmem(row, 8, length, dtype=F32),
        vmem(row, 8, length, dtype=F32),
        vmem(row, 8, length, dtype=F32),
        vmem(row, 8, length, dtype=F32),
        vmem(row, LANES, dtype=F32),
    ]
    one, many = pltpu.SemaphoreType.DMA, lambda n: pltpu.SemaphoreType.DMA((n,))
    semaphores = [
        one, one,
        one, one,
        one, many(row),
        one, many(row),
        one, many(row),
        one, many(row),
        one, many(row),
        one, many(slabs),
        one, many(slabs),
        one, many(slabs),
        one, one,
        one, one,
        one, many(row),
        one, many(row),
        one, many(row),
        one, one,
        one, one,
        one, one,
        one, one,
        many(9),
    ]
    in_vmem = pl.BlockSpec(memory_space=pltpu.VMEM)
    in_hbm = pl.BlockSpec(memory_space=pltpu.HBM)
    like = jax.ShapeDtypeStruct
    results = pl.pallas_call(
        functools.partial(kernel, (slabs, row, zs, heads)),
        out_shape=[
            like((2, TOK, inner), BF16),
            like((2, TOK, zs * STATE), BF16),
            like((TOK, heads), BF16),
            like((8, LANES), F32),
        ],
        in_specs=[in_hbm] * 9,
        out_specs=[in_vmem] * 4,
        scratch_shapes=scratch + semaphores,
        compiler_params=pltpu.CompilerParams(
            collective_id=0, has_side_effects=True, vmem_limit_bytes=62 * 2**20
        ),
        name="scan_backward",
    )(x_proj, z_gate, out_grad, b_proj, c_proj, dt_raw, dt_bias, a_log, d_skip)
    anywhere = pl.BlockSpec(memory_space=pl.ANY)
    return pl.pallas_call(
        unpack,
        out_shape=[
            like((TOK, inner), BF16),
            like((TOK, inner), BF16),
            like((TOK, zs * STATE), BF16),
            like((TOK, zs * STATE), BF16),
            like((TOK, heads), BF16),
            like((per,), F32),
            like((per,), F32),
            like((per,), F32),
        ],
        in_specs=[anywhere] * 3 + [in_vmem],
        out_specs=[anywhere] * 5 + [in_vmem] * 3,
        scratch_shapes=[
            vmem(2, TOK, inner),
            vmem(2, TOK, zs * STATE),
            vmem(TOK, heads),
            many(5),
            many(5),
        ],
        compiler_params=pltpu.CompilerParams(vmem_limit_bytes=62 * 2**20),
        name="unpack",
    )(*results)


def solution(mesh, row=ROW):
    tokens = P(("seq", "head"), None)
    return jax.shard_map(
        functools.partial(shards, row),
        mesh=mesh,
        in_specs=(tokens,) * 6 + (P("head"),) * 3,
        out_specs=(tokens,) * 5 + (P("head"),) * 3,
        check_vma=False,
    )
```

```python
import functools

import jax
import jax.numpy as jnp
from jax import lax
from jax.experimental import pallas as pl
from jax.experimental.pallas import tpu as pltpu
from jax.sharding import PartitionSpec as P

ROW = 8
TOK = 16
PARTS = 4
WIDE = 2
STATE = 128
LANES = 128
HALF = 64

F32 = jnp.float32
BF16 = jnp.bfloat16
MESH = pl.DeviceIdType.MESH


def mm(a, b, ca, cb):
    return lax.dot_general(a, b, (((ca,), (cb,)), ((), ())), preferred_element_type=F32)


def mm_exact(a, b):
    return lax.dot_general(
        a,
        b,
        (((1,), (0,)), ((), ())),
        precision=lax.Precision.HIGHEST,
        preferred_element_type=F32,
    )


def loop(low, high, body):
    def step(i, carry):
        body(i)
        return carry

    lax.fori_loop(low, high, step, 0)


def pairs(count, body, after=None):
    def step(k):
        for i in range(WIDE):
            body(k * WIDE + i)
        if after is not None:
            for i in range(WIDE):
                after(k * WIDE + i)

    loop(0, count // WIDE, step)


def bytes_wait(ref, sem):
    pltpu.make_async_copy(ref, ref, sem).wait()


def kernel(
    sizes,
    x_hbm, z_hbm, og_hbm, b_hbm, c_hbm, dt_hbm, bias_hbm, alog_hbm, skip_hbm,
    inner_hbm, outer_hbm, gdt_hbm, sums_hbm,
    x_ref, z_ref, og_ref, b_ref, c_ref, dt_ref, bias_ref, alog_ref, skip_ref,
    sx, sg, rx, rg, sbc, rzb, scz, rcz, rb, rc, sdt, rdt, ssend, asend, srecv, arecv, skept, rkept, fades, sy, sdx, ry, rdx,
    sdb, sdc, mdb, mdc, tdb, tdc, rdb, rdc, sgd, rgd, szo, rzo, szc, rzc, ssy, rsy, ssr, rsr,
    inner_ref, outer_ref, gdt_ref, sums_ref, slope, turn, cols, ecol, wcol, eg, wx, st_s, st_a, hb, gb, affs, decs, scores,
    y_in, dx_in, dc_in, db_in, ds0, dla0, rho, kap, cterm, skipsum,
    zb_send, zb_recv, zc_send, zc_recv, x_send, x_recv, g_send, g_recv, b_send, b_recv, c_send, c_recv,
    dt_send, dt_recv, s_send, s_recv, a_send, a_recv, k_send, k_recv, y_send, y_recv, dx_send, dx_recv,
    db_send, db_recv, dc_send, dc_recv, mb_send, mb_recv, mc_send, mc_recv, gd_send, gd_recv, zo_send, zo_recv, oc_send, oc_recv,
    sy_send, sy_recv, sr_send, sr_recv, load, done,
):
    slabs, row, zs, heads = sizes
    length = zs * TOK
    per = 2 * row
    seq, z = lax.axis_index("seq"), lax.axis_index("head")
    y, r = lax.div(seq, row), lax.rem(seq, row)
    low = y < slabs // 2
    mine = pl.ds(pl.multiple_of(z * TOK, TOK), TOK)

    def either(early, late):
        pl.when(low)(early)
        pl.when(jnp.logical_not(low))(late)

    def at(row_to, z_to):
        return (y * row + row_to, z_to)

    def other(i):
        return lax.rem(r + lax.div(i, zs), row), lax.rem(z + lax.rem(i, zs), zs)

    def lanes_of(d):
        return pl.ds(pl.multiple_of(d * LANES, LANES), LANES)

    def tokens_of(k):
        return pl.ds(pl.multiple_of(k * TOK, TOK), TOK)

    def send(src, dst, send_sem, recv_sem, device):
        pltpu.make_async_remote_copy(
            src_ref=src,
            dst_ref=dst,
            send_sem=send_sem,
            recv_sem=recv_sem,
            device_id=device,
            device_id_type=MESH,
        ).start()

    def keep(src, dst, recv_sem):
        pltpu.make_async_copy(src, dst, recv_sem).start()

    barrier = pltpu.get_barrier_semaphore()

    def greet(i):
        pl.semaphore_signal(barrier, inc=1, device_id=at(*other(i)), device_id_type=MESH)

    def greet_slab(i):
        there = (lax.rem(y + i, slabs) * row + r, z)
        pl.semaphore_signal(barrier, inc=1, device_id=there, device_id_type=MESH)

    loop(1, row * zs, greet)
    loop(1, slabs, greet_slab)

    loads = [
        pltpu.make_async_copy(there, here, load.at[i])
        for i, (there, here) in enumerate(
            (
                (b_hbm, b_ref),
                (c_hbm, c_ref),
                (dt_hbm, dt_ref),
                (x_hbm, x_ref),
                (z_hbm, z_ref),
                (og_hbm, og_ref),
                (bias_hbm, bias_ref),
                (alog_hbm, alog_ref),
                (skip_hbm, skip_ref),
            )
        )
    ]
    for copy in loads:
        copy.start()

    for copy in loads[:3]:
        copy.wait()
    def pack(one_ref, two_ref):
        for k in range(zs):
            sbc[k, 0] = one_ref[:, k * STATE : (k + 1) * STATE]
            scz[k] = two_ref[:, k * STATE : (k + 1) * STATE]

    either(lambda: pack(b_ref, c_ref), lambda: pack(c_ref, b_ref))
    for k in range(zs):
        sbc[k, 1, :, 0:heads] = dt_ref[...]
    loads[3].wait()
    for d in range(row * zs):
        sx[d] = x_ref[:, d * LANES : (d + 1) * LANES]
    pl.semaphore_wait(barrier, row * zs - 1 + slabs - 1)

    keep(sbc.at[z], rzb.at[:, mine, :], zb_recv)

    def send_zb(i):
        to = lax.rem(z + i, zs)
        send(sbc.at[to], rzb.at[:, mine, :], zb_send, zb_recv, at(r, to))

    loop(1, zs, send_zb)

    def send_x(i):
        r_to, z_to = other(i)
        d = z_to * row + r_to
        send(sx.at[d], rx.at[r, mine, :], x_send, x_recv.at[r], at(r_to, z_to))

    def all_x():
        keep(sx.at[z * row + r], rx.at[r, mine, :], x_recv.at[r])
        loop(1, row * zs, send_x)

    def gate(k):
        for i in range(row):
            d = k * row + i
            zf, of = z_ref[:, lanes_of(d)].astype(F32), og_ref[:, lanes_of(d)].astype(F32)
            s = jax.nn.sigmoid(zf)
            sg[d] = (of * (zf * s)).astype(BF16)
            slope[d] = of * (s * (1.0 + zf * (1.0 - s)))

    def send_g(i):
        r_to, z_to = other(i)
        d = z_to * row + r_to
        send(sg.at[d], rg.at[r, mine, :], g_send, g_recv.at[r], at(r_to, z_to))

    def all_g():
        for copy in loads[4:6]:
            copy.wait()
        loop(0, zs, gate)
        keep(sg.at[z * row + r], rg.at[r, mine, :], g_recv.at[r])
        loop(1, row * zs, send_g)

    either(all_x, all_g)

    keep(scz.at[z], rcz.at[mine, :], zc_recv)

    def send_zc(i):
        to = lax.rem(z + i, zs)
        send(scz.at[to], rcz.at[mine, :], zc_send, zc_recv, at(r, to))

    loop(1, zs, send_zc)

    def share(src, dst, send_sem, recv_sem):
        keep(src, dst.at[r], recv_sem.at[r])

        def one(i):
            to = lax.rem(r + i, row)
            send(src, dst.at[r], send_sem, recv_sem.at[r], at(to, z))

        loop(1, row, one)

    bytes_wait(rzb, zb_recv)
    either(
        lambda: share(rzb.at[0], rb, b_send, b_recv), lambda: share(rzb.at[0], rc, c_send, c_recv)
    )

    for copy in loads[6:]:
        copy.wait()
    turn[...] = jnp.transpose(rzb[1].astype(F32)[:, 0:heads])
    raw = turn[pl.ds(pl.multiple_of(z * per, per), per), :]
    head_at = lax.broadcasted_iota(jnp.int32, (per, length), 0)
    token_at = lax.broadcasted_iota(jnp.int32, (per, length), 1)
    bias = jnp.zeros((per, length), F32)
    rate = jnp.zeros((per, length), F32)
    for h in range(per):
        bias = jnp.where(head_at == h, bias_ref[h], bias)
        rate = jnp.where(head_at == h, alog_ref[h], rate)
    pre = raw + bias
    step = jnp.maximum(pre, 0.0) + jnp.log1p(jnp.exp(-jnp.abs(pre)))
    squash = jax.nn.sigmoid(pre)
    decay = -jnp.exp(rate) * step
    cum = decay
    reach = 1
    while reach < length:
        cum = cum + jnp.where(token_at >= reach, pltpu.roll(cum, reach, 1), 0.0)
        reach *= 2
    for d in range(row):
        pair = slice(2 * d, 2 * d + 2)
        sdt[d] = jnp.concatenate([step[pair], cum[pair], squash[pair], decay[pair]], axis=0)
    keep(sdt.at[r], rdt.at[r], dt_recv.at[r])

    def send_dt(i):
        to = lax.rem(r + i, row)
        send(sdt.at[to], rdt.at[r], dt_send, dt_recv.at[r], at(to, z))

    loop(1, row, send_dt)

    either(all_g, all_x)
    bytes_wait(rcz, zc_recv)
    either(lambda: share(rcz, rc, c_send, c_recv), lambda: share(rcz, rb, b_send, b_recv))

    lane = lax.broadcasted_iota(jnp.int32, (1, LANES), 1)
    first = lane < HALF
    sel = [first.astype(F32), 1.0 - first.astype(F32)]
    skip = jnp.where(first, skip_ref[2 * r], skip_ref[2 * r + 1])
    at_row = lax.broadcasted_iota(jnp.int32, (length, length), 0)
    at_col = lax.broadcasted_iota(jnp.int32, (length, length), 1)
    causal = at_row >= at_col
    before = (at_row < at_col).astype(F32)
    sel_at = lax.broadcasted_iota(jnp.int32, (16, LANES), 0)
    sel_lane = lax.broadcasted_iota(jnp.int32, (16, LANES), 1)
    pick = jnp.where(sel_at == lax.div(sel_lane, HALF), 1.0, 0.0)
    pick16 = pick.astype(BF16)

    def chunk(k):
        return lax.rem(r + row - k, row)

    def last_decay(c):
        return fades[c, 0:1]

    def decays_of(k):
        c = chunk(k)
        rows = rdt[c]
        across = jnp.transpose(rows)
        cols[c] = across
        up = jnp.where(first, across[:, 2:3], across[:, 3:4])
        end = jnp.where(first, rows[2:3, length - 1 :], rows[3:4, length - 1 :])
        size = jnp.where(first, across[:, 0:1], across[:, 1:2])
        ecol[c] = jnp.exp(up)
        wcol[c] = jnp.exp(end - up) * size
        fades[c] = jnp.broadcast_to(jnp.exp(end), (8, LANES))

    loop(0, row, lambda c: bytes_wait(rdt.at[c], dt_recv.at[c]))
    pairs(row, decays_of)
    kept = fades[0]
    for c in range(1, row):
        kept = kept * fades[c]
    skept[...] = kept

    def send_kept(i):
        there = (lax.rem(y + i, slabs) * row + r, z)
        send(skept, rkept.at[y], k_send, k_recv.at[y], there)

    loop(1, slabs, send_kept)

    def states(k):
        c = chunk(k)
        bytes_wait(rx.at[c], x_recv.at[c])
        grown = (wcol[c] * rx[c].astype(F32)).astype(BF16)
        wx[c] = grown
        st_s[c] = mm(rb[c], grown, 0, 0)

    def send_s(i):
        @pl.when(y + i < slabs)
        def _():
            send(ssend, srecv.at[y], s_send, s_recv.at[y], ((y + i) * row + r, z))

    def states_out():
        loop(0, row, lambda c: bytes_wait(rb.at[c], b_recv.at[c]))
        states_late()

    def states_late():
        loop(0, row, states)
        state = jnp.zeros((STATE, LANES), F32)
        for c in range(row):
            state = last_decay(c) * state + st_s[c]
        ssend[...] = state.astype(BF16)
        loop(1, slabs, send_s)

    def cotangents(k):
        c = chunk(k)
        bytes_wait(rg.at[c], g_recv.at[c])
        faded = (ecol[c] * rg[c].astype(F32)).astype(BF16)
        eg[c] = faded
        st_a[c] = mm(rc[c], faded, 0, 0)

    def send_a(i):
        @pl.when(y >= i)
        def _():
            send(asend, arecv.at[y], a_send, a_recv.at[y], ((y - i) * row + r, z))

    def cotangents_out():
        loop(0, row, lambda c: bytes_wait(rc.at[c], c_recv.at[c]))
        cotangents_late()

    def cotangents_late():
        loop(0, row, cotangents)
        back = jnp.zeros((STATE, LANES), F32)
        for c in reversed(range(row)):
            back = last_decay(c) * back + st_a[c]
        asend[...] = back.astype(BF16)
        loop(1, slabs, send_a)

    def inner_y(c):
        xf = rx[c].astype(F32)
        total = skip * xf
        for j in range(2):
            total = total + mm(scores[c, j], (xf * sel[j]).astype(BF16), 1, 0)
        y_in[c] = total

    def inner_x(c):
        gf = rg[c].astype(F32)
        total = skip * gf
        for j in range(2):
            total = total + mm(scores[c, j], (gf * sel[j]).astype(BF16), 0, 0)
        dx_in[c] = total

    def scored(then, k):
        c = chunk(k)
        across = cols[c]
        aff = mm(rc[c], rb[c], 1, 1)
        affs[c] = aff
        for j in range(2):
            fall = across[:, 2 + j : 3 + j] - rdt[c, 2 + j : 3 + j, :]
            e = jnp.where(causal, jnp.exp(fall), 0.0)
            decs[c, j] = e
            scores[c, j] = (e * aff * rdt[c, j : j + 1, :]).astype(BF16)
        then(c)

    def await_kept():
        def one(i):
            source = lax.rem(y + i, slabs)
            bytes_wait(rkept.at[source], k_recv.at[source])

        loop(1, slabs, one)

    def states_in():
        state = jnp.zeros((STATE, LANES), F32)
        for i in reversed(range(1, slabs)):
            source = lax.rem(y + slabs - i, slabs)

            @pl.when(y >= i)
            def _():
                bytes_wait(srecv.at[source], s_recv.at[source])

            fade = rkept[source, 0:1]
            state = jnp.where(y >= i, fade * state + srecv[source].astype(F32), state)
        for c in range(row):
            hb[c] = state.astype(BF16)
            here = st_s[c]
            st_s[c] = state
            state = last_decay(c) * state + here

    def cotangents_in():
        back = jnp.zeros((STATE, LANES), F32)
        for i in reversed(range(1, slabs)):
            source = lax.rem(y + i, slabs)

            @pl.when(y + i < slabs)
            def _():
                bytes_wait(arecv.at[source], a_recv.at[source])

            fade, part = rkept[source, 0:1], arecv[source].astype(F32)
            back = jnp.where(y + i < slabs, fade * back + part, back)
        for c in reversed(range(row)):
            gb[c] = back.astype(BF16)
            here = st_a[c]
            st_a[c] = back
            back = last_decay(c) * back + here

    there = z * row + r

    def leave(buffer, landing, send_sem, recv_sem, k):
        c = lax.rem(r + k, row)

        @pl.when(k == 0)
        def _():
            keep(buffer.at[c, mine, :], landing.at[there], recv_sem)

        @pl.when(k > 0)
        def _():
            send(buffer.at[c, mine, :], landing.at[there], send_sem, recv_sem, at(c, z))

        def one(i):
            to = lax.rem(z + i, zs)
            part = buffer.at[c, tokens_of(to), :]
            send(part, landing.at[there], send_sem, recv_sem, at(c, to))

        loop(1, zs, one)

    leave_y = functools.partial(leave, sy, ry, y_send, y_recv)
    leave_x = functools.partial(leave, sdx, rdx, dx_send, dx_recv)

    half, mate = row // 2, lax.rem(r, 2)
    chip = lax.div(r, 2)

    def to_mate(buffer, landing, send_sem, recv_sem):
        def one(i):
            src = buffer.at[2 * i + 1 - mate]
            send(src, landing.at[i], send_sem, recv_sem.at[i], at(r + 1 - 2 * mate, z))

        loop(0, half, one)

    def to_chips(buffer, landing, recv_sem, summed, final, out_sem, in_sem):
        def one(k):
            i = lax.rem(chip + k, half)
            c = 2 * i + mate
            bytes_wait(landing.at[i], recv_sem.at[i])
            summed[i] = (buffer[c].astype(F32) + landing[i].astype(F32)).astype(BF16)

            @pl.when(k == 0)
            def _():
                keep(summed.at[i], final.at[chip], in_sem.at[chip])

            @pl.when(k > 0)
            def _():
                send(summed.at[i], final.at[chip], out_sem, in_sem.at[chip], at(c, z))

        loop(0, half, one)

    c_to_mate = functools.partial(to_mate, sdc, mdc, mc_send, mc_recv)
    b_to_mate = functools.partial(to_mate, sdb, mdb, mb_send, mb_recv)
    c_to_chips = functools.partial(to_chips, sdc, mdc, mc_recv, tdc, rdc, dc_send, dc_recv)
    b_to_chips = functools.partial(to_chips, sdb, mdb, mb_recv, tdb, rdb, db_send, db_recv)

    def finish_y(k):
        c = lax.rem(r + k, row)
        yi = ecol[c] * mm(rc[c], hb[c], 1, 0)
        sy[c] = (y_in[c] + yi).astype(BF16)
        rho[c] = mm(pick16, (rg[c].astype(F32) * yi).astype(BF16), 1, 1)[0:8]

    def finish_x(k):
        c = lax.rem(r + k, row)
        bi = wcol[c] * mm(rb[c], gb[c], 1, 0)
        sdx[c] = (dx_in[c] + bi).astype(BF16)
        kap[c] = mm(pick16, (rx[c].astype(F32) * bi).astype(BF16), 1, 1)[0:8]

    def finish_c(k):
        c = lax.rem(r + k, row)
        sdc[c] = (dc_in[c] + mm(eg[c], hb[c], 1, 1)).astype(BF16)

    def finish_b(k):
        c = lax.rem(r + k, row)
        sdb[c] = (db_in[c] + mm(wx[c], gb[c], 1, 1)).astype(BF16)

    def pulled(then, k):
        c = lax.rem(r + k, row)
        xs, gs = rx[c], rg[c]
        xf, gf = xs.astype(F32), gs.astype(F32)
        aff = affs[c]
        pulls = jnp.zeros((length, length), F32)
        for j in range(2):
            size = rdt[c, j : j + 1, :]
            k1 = decs[c, j] * mm((gf * sel[j]).astype(BF16), xs, 1, 1)
            k0 = k1 * aff
            ds0[c, j : j + 1, :] = jnp.sum(k0, axis=0, keepdims=True)
            crossing = mm((k0 * size).astype(BF16), before.astype(BF16), 1, 0)
            dla0[c, j : j + 1, :] = jnp.sum(
                jnp.where(causal, crossing, 0.0), axis=0, keepdims=True
            )
            pulls = pulls + k1 * size
        pulls = pulls.astype(BF16)
        dc_in[c] = mm(pulls, rb[c], 1, 0)
        db_in[c] = mm(pulls, rc[c], 0, 0)
        skipsum[pl.ds(c, 1), :] = jnp.sum(xf * gf, axis=0, keepdims=True)
        then(c)

    def added(landing, recv_sem):
        loop(0, half, lambda c: bytes_wait(landing.at[c], recv_sem.at[c]))
        total = landing[0].astype(F32)
        for c in range(1, half):
            total = total + landing[c].astype(F32)
        return total.astype(BF16)

    def send_oc(i):
        to = lax.rem(z + i, zs)
        send(szc.at[tokens_of(to), :], rzc.at[z], oc_send, oc_recv, at(r, to))

    def small_out(landing, recv_sem):
        szc[...] = added(landing, recv_sem)
        keep(szc.at[mine, :], rzc.at[z], oc_recv)
        loop(1, zs, send_oc)

    def both(k, one, two):
        one(k)
        two(k)

    def x_first():
        states_out()
        loop(0, row, lambda c: bytes_wait(rc.at[c], c_recv.at[c]))
        pairs(row, functools.partial(scored, inner_y))
        cotangents_late()
        await_kept()
        states_in()
        pairs(row, finish_y, leave_y)
        pairs(row, functools.partial(pulled, inner_x))
        pairs(row, finish_c)
        c_to_mate()
        cotangents_in()
        c_to_chips()
        pairs(row, lambda k: both(k, finish_x, finish_b))
        b_to_mate()

    def g_first():
        cotangents_out()
        loop(0, row, lambda c: bytes_wait(rb.at[c], b_recv.at[c]))
        pairs(row, functools.partial(scored, inner_x))
        states_late()
        await_kept()
        cotangents_in()
        pairs(row, finish_x, leave_x)
        pairs(row, functools.partial(pulled, inner_y))
        pairs(row, finish_b)
        b_to_mate()
        states_in()
        b_to_chips()
        pairs(row, lambda k: both(k, finish_y, finish_c))
        c_to_mate()

    either(x_first, g_first)
    for c in range(row):
        over = last_decay(c) * jnp.sum(st_s[c] * st_a[c], axis=0, keepdims=True)
        cterm[c] = jnp.broadcast_to(
            jnp.sum(pick[0:8] * over, axis=1, keepdims=True), (8, length)
        )

    flat = (row * 8, length)
    dla = (
        dla0[...].reshape(flat)
        + mm_exact(rho[...].reshape(flat), causal.astype(F32))
        + mm_exact(kap[...].reshape(flat), before)
        + cterm[...].reshape(flat)
    )
    parts = [rdt[c] for c in range(row)]
    steps = jnp.concatenate(parts, axis=0)
    squashes = jnp.concatenate([pltpu.roll(p, 4, 0) for p in parts], axis=0)
    decays = jnp.concatenate([pltpu.roll(p, 2, 0) for p in parts], axis=0)
    which = lax.rem(lax.broadcasted_iota(jnp.int32, flat, 0), 8)
    rates = jnp.exp(jnp.where(which == 0, alog_ref[2 * r], alog_ref[2 * r + 1]))
    dsteps = ds0[...].reshape(flat) + kap[...].reshape(flat) / steps - rates * dla
    draws = jnp.where(which < 2, dsteps * squashes, 0.0)
    dlogs = jnp.where(which < 2, dla * decays, 0.0)
    sgd[...] = draws.reshape(row, 8, length)
    keep(sgd.at[r], rgd.at[r], gd_recv.at[r])

    def send_gd(i):
        to = lax.rem(r + i, row)
        send(sgd.at[to], rgd.at[r], gd_send, gd_recv.at[r], at(to, z))

    loop(1, row, send_gd)

    sum_at = lax.broadcasted_iota(jnp.int32, (8, LANES), 0)
    sum_lane = lax.broadcasted_iota(jnp.int32, (8, LANES), 1)
    sums = jnp.zeros((8, LANES), F32)
    for j in range(2):
        totals = (
            jnp.sum(jnp.where(which == j, draws, 0.0)),
            jnp.sum(jnp.where(which == j, dlogs, 0.0)),
            jnp.sum(skipsum[...] * sel[j]),
        )
        for q in range(3):
            place = (sum_at == q) & (sum_lane == 2 * r + j)
            sums = jnp.where(place, totals[q], sums)
    ssy[...] = sums
    keep(ssy, rsy.at[y], sy_recv)

    def send_sy(i):
        send(ssy, rsy.at[y], sy_send, sy_recv, (lax.rem(y + i, slabs) * row + r, z))

    loop(1, slabs, send_sy)

    def x_out():
        loop(0, row, leave_x)
        b_to_chips()
        small_out(rdc, dc_recv)

    def y_out():
        loop(0, row, leave_y)
        c_to_chips()
        small_out(rdb, db_recv)

    either(x_out, y_out)

    def late_sum(landing, recv_sem):
        szo[0] = added(landing, recv_sem)

    either(lambda: late_sum(rdb, db_recv), lambda: late_sum(rdc, dc_recv))
    loop(0, row, lambda c: bytes_wait(rgd.at[c], gd_recv.at[c]))
    turn[...] = jnp.zeros_like(turn)
    turn[pl.ds(pl.multiple_of(z * per, per), per), :] = jnp.concatenate(
        [rgd[c][0:2] for c in range(row)], axis=0
    )
    szo[1, :, 0:heads] = jnp.transpose(turn[...]).astype(BF16)
    keep(szo.at[:, mine, :], rzo.at[z], zo_recv)

    def send_zo(i):
        to = lax.rem(z + i, zs)
        send(szo.at[:, tokens_of(to), :], rzo.at[z], zo_send, zo_recv, at(r, to))

    loop(1, zs, send_zo)

    bytes_wait(rsy, sy_recv)
    total = rsy[0]
    for i in range(1, slabs):
        total = total + rsy[i]
    ssr[...] = total
    keep(ssr, rsr.at[r], sr_recv)

    def send_sr(i):
        send(ssr, rsr.at[r], sr_send, sr_recv, at(lax.rem(r + i, row), z))

    loop(1, row, send_sr)

    results = [
        pltpu.make_async_copy(inner_ref.at[0], inner_hbm.at[0], done.at[0]),
        pltpu.make_async_copy(inner_ref.at[1], inner_hbm.at[1], done.at[1]),
        pltpu.make_async_copy(outer_ref, outer_hbm, done.at[2]),
        pltpu.make_async_copy(gdt_ref, gdt_hbm, done.at[3]),
        pltpu.make_async_copy(sums_ref, sums_hbm, done.at[4]),
    ]

    def gate_back(k):
        for i in range(row):
            d = k * row + i
            inner_ref[1, :, lanes_of(d)] = (slope[d] * ry[d].astype(F32)).astype(BF16)

    def take_y():
        bytes_wait(ry, y_recv)
        loop(0, zs, gate_back)
        results[1].start()

    def take_x():
        bytes_wait(rdx, dx_recv)
        for d in range(row * zs):
            inner_ref[0, :, d * LANES : (d + 1) * LANES] = rdx[d]
        results[0].start()

    def take_small(early, late):
        bytes_wait(rzc, oc_recv)
        for k in range(zs):
            outer_ref[early, :, k * STATE : (k + 1) * STATE] = rzc[k]
        bytes_wait(rzo, zo_recv)
        for k in range(zs):
            outer_ref[late, :, k * STATE : (k + 1) * STATE] = rzo[k, 0]

    def x_last():
        take_y()
        take_x()
        take_small(1, 0)

    def y_last():
        take_x()
        take_y()
        take_small(0, 1)

    either(x_last, y_last)
    total = jnp.zeros((TOK, heads), F32)
    for k in range(zs):
        total = total + rzo[k, 1, :, 0:heads].astype(F32)
    gdt_ref[...] = total.astype(BF16)
    results[2].start()
    results[3].start()
    bytes_wait(rsr, sr_recv)
    total = rsr[0]
    for i in range(1, row):
        total = total + rsr[i]
    sums_ref[...] = total
    results[4].start()

    for copy in results:
        copy.wait()
    @pl.when(y < slabs - 1)
    def _():
        loop(0, slabs - 1 - y, lambda i: bytes_wait(ssend, s_send))

    @pl.when(y > 0)
    def _():
        loop(0, y, lambda i: bytes_wait(asend, a_send))

    blocks = sg.at[pl.ds(0, row * zs - 1)]
    for sem in (x_send, g_send, y_send, dx_send):
        bytes_wait(blocks, sem)
    others = pl.ds(0, row - 1)
    bytes_wait(sbc.at[pl.ds(0, zs - 1)], zb_send)
    bytes_wait(scz.at[pl.ds(0, zs - 1)], zc_send)
    bytes_wait(rb.at[others], b_send)
    bytes_wait(rc.at[others], c_send)
    bytes_wait(sdt.at[others], dt_send)
    chips = pl.ds(0, half - 1)
    bytes_wait(rdb.at[chips], db_send)
    bytes_wait(rdc.at[chips], dc_send)
    bytes_wait(mdb, mb_send)
    bytes_wait(mdc, mc_send)
    bytes_wait(sgd.at[others], gd_send)
    bytes_wait(rzo.at[pl.ds(0, zs - 1)], zo_send)
    bytes_wait(rzc.at[pl.ds(0, zs - 1)], oc_send)
    bytes_wait(rsy.at[pl.ds(0, slabs - 1)], sy_send)
    bytes_wait(rsr.at[others], sr_send)
    bytes_wait(rkept.at[pl.ds(0, slabs - 1)], k_send)


def unpack(
    inner_hbm, outer_hbm, dt_hbm, sums_hbm,
    gx_ref, gz_ref, gb_ref, gc_ref, gdt_ref, bias_ref, alog_ref, skip_ref,
    inner, outer, dts, sums, bias, alog, skip, come, go,
):
    width = gx_ref.shape[1] // PARTS
    moves = []
    for q, ref in enumerate((gx_ref, gz_ref)):
        for p in range(PARTS):
            part = pl.ds(p * width, width)
            moves.append((inner_hbm.at[q, :, part], inner.at[q, :, part], ref.at[:, part]))
    moves += [
        (outer_hbm.at[0], outer.at[0], gb_ref),
        (outer_hbm.at[1], outer.at[1], gc_ref),
        (dt_hbm, dts, gdt_ref),
    ]
    came = [pltpu.make_async_copy(a, b, come.at[i]) for i, (a, b, _) in enumerate(moves)]
    gone = [pltpu.make_async_copy(b, c, go.at[i]) for i, (_, b, c) in enumerate(moves)]
    last = len(moves)
    came_sums = pltpu.make_async_copy(sums_hbm, sums, come.at[last])
    came_sums.start()
    for copy in came:
        copy.start()
    came_sums.wait()
    for q, (row, ref) in enumerate(((bias, bias_ref), (alog, alog_ref), (skip, skip_ref))):
        row[...] = sums[q, 0 : row.shape[0]]
        gone.append(pltpu.make_async_copy(row, ref, go.at[last + q]))
        gone[-1].start()
    for first, second in zip(came, gone[:last]):
        first.wait()
        second.start()
    for copy in gone:
        copy.wait()


def shards(row, x_proj, z_gate, out_grad, b_proj, c_proj, dt_raw, dt_bias, a_log, d_skip):
    zs = lax.axis_size("head")
    slabs = lax.axis_size("seq") // row
    heads = 2 * row * zs
    length = zs * TOK
    inner = heads * HALF

    def vmem(*shape, dtype=BF16):
        return pltpu.VMEM(shape, dtype)

    square = (row, length, LANES)
    half = (row // 2, length, LANES)
    states = (row, STATE, LANES)
    per = 2 * row
    scratch = [
        vmem(TOK, inner),
        vmem(TOK, inner),
        vmem(TOK, inner),
        vmem(TOK, zs * STATE),
        vmem(TOK, zs * STATE),
        vmem(TOK, heads),
        pltpu.SMEM((per,), F32),
        pltpu.SMEM((per,), F32),
        pltpu.SMEM((per,), F32),
        vmem(row * zs, TOK, LANES),
        vmem(row * zs, TOK, LANES),
        vmem(*square),
        vmem(*square),
        vmem(zs, 2, TOK, STATE),
        vmem(2, length, STATE),
        vmem(zs, TOK, STATE),
        vmem(length, STATE),
        vmem(*square),
        vmem(*square),
        vmem(row, 8, length, dtype=F32),
        vmem(row, 8, length, dtype=F32),
        vmem(STATE, LANES),
        vmem(STATE, LANES),
        vmem(slabs, STATE, LANES),
        vmem(slabs, STATE, LANES),
        vmem(8, LANES, dtype=F32),
        vmem(slabs, 8, LANES, dtype=F32),
        vmem(row, 8, LANES, dtype=F32),
        vmem(*square),
        vmem(*square),
        vmem(row * zs, TOK, LANES),
        vmem(row * zs, TOK, LANES),
        vmem(*square),
        vmem(*square),
        vmem(*half),
        vmem(*half),
        vmem(*half),
        vmem(*half),
        vmem(*half),
        vmem(*half),
        vmem(row, 8, length, dtype=F32),
        vmem(row, 8, length, dtype=F32),
        vmem(2, length, STATE),
        vmem(zs, 2, TOK, STATE),
        vmem(length, STATE),
        vmem(zs, TOK, STATE),
        vmem(8, LANES, dtype=F32),
        vmem(slabs, 8, LANES, dtype=F32),
        vmem(8, LANES, dtype=F32),
        vmem(row, 8, LANES, dtype=F32),
        vmem(2, TOK, inner),
        vmem(2, TOK, zs * STATE),
        vmem(TOK, heads),
        vmem(8, LANES, dtype=F32),
        vmem(row * zs, TOK, LANES, dtype=F32),
        vmem(heads, length, dtype=F32),
        vmem(row, length, 8, dtype=F32),
        vmem(*square, dtype=F32),
        vmem(*square, dtype=F32),
        vmem(*square),
        vmem(*square),
        vmem(*states, dtype=F32),
        vmem(*states, dtype=F32),
        vmem(*states),
        vmem(*states),
        vmem(row, length, length, dtype=F32),
        vmem(row, 2, length, length, dtype=F32),
        vmem(row, 2, length, length),
        vmem(*square, dtype=F32),
        vmem(*square, dtype=F32),
        vmem(*square, dtype=F32),
        vmem(*square, dtype=F32),
        vmem(row, 8, length, dtype=F32),
        vmem(row, 8, length, dtype=F32),
        vmem(row, 8, length, dtype=F32),
        vmem(row, 8, length, dtype=F32),
        vmem(row, 8, length, dtype=F32),
        vmem(row, LANES, dtype=F32),
    ]
    one, many = pltpu.SemaphoreType.DMA, lambda n: pltpu.SemaphoreType.DMA((n,))
    semaphores = [
        one, one,
        one, one,
        one, many(row),
        one, many(row),
        one, many(row),
        one, many(row),
        one, many(row),
        one, many(slabs),
        one, many(slabs),
        one, many(slabs),
        one, one,
        one, one,
        one, many(row // 2),
        one, many(row // 2),
        one, many(row // 2),
        one, many(row // 2),
        one, many(row),
        one, one,
        one, one,
        one, one,
        one, one,
        many(9),
        many(5),
    ]
    in_hbm = pl.BlockSpec(memory_space=pltpu.HBM)
    like = jax.ShapeDtypeStruct
    results = pl.pallas_call(
        functools.partial(kernel, (slabs, row, zs, heads)),
        out_shape=[
            like((2, TOK, inner), BF16),
            like((2, TOK, zs * STATE), BF16),
            like((TOK, heads), BF16),
            like((8, LANES), F32),
        ],
        in_specs=[in_hbm] * 9,
        out_specs=[in_hbm] * 4,
        scratch_shapes=scratch + semaphores,
        compiler_params=pltpu.CompilerParams(
            collective_id=0, has_side_effects=True, vmem_limit_bytes=62 * 2**20
        ),
        name="scan_backward",
    )(x_proj, z_gate, out_grad, b_proj, c_proj, dt_raw, dt_bias, a_log, d_skip)
    anywhere = pl.BlockSpec(memory_space=pl.ANY)
    return pl.pallas_call(
        unpack,
        out_shape=[
            like((TOK, inner), BF16),
            like((TOK, inner), BF16),
            like((TOK, zs * STATE), BF16),
            like((TOK, zs * STATE), BF16),
            like((TOK, heads), BF16),
            like((per,), F32),
            like((per,), F32),
            like((per,), F32),
        ],
        in_specs=[anywhere] * 4,
        out_specs=[anywhere] * 8,
        scratch_shapes=[
            vmem(2, TOK, inner),
            vmem(2, TOK, zs * STATE),
            vmem(TOK, heads),
            vmem(8, LANES, dtype=F32),
            vmem(per, dtype=F32),
            vmem(per, dtype=F32),
            vmem(per, dtype=F32),
            many(2 * PARTS + 4),
            many(2 * PARTS + 6),
        ],
        compiler_params=pltpu.CompilerParams(vmem_limit_bytes=62 * 2**20),
        name="unpack",
    )(*results)


def solution(mesh, row=ROW):
    tokens = P(("seq", "head"), None)
    return jax.shard_map(
        functools.partial(shards, row),
        mesh=mesh,
        in_specs=(tokens,) * 6 + (P("head"),) * 3,
        out_specs=(tokens,) * 5 + (P("head"),) * 3,
        check_vma=False,
    )
```

```python
import functools

import jax
import jax.numpy as jnp
from jax import lax
from jax.experimental import pallas as pl
from jax.experimental.pallas import tpu as pltpu
from jax.sharding import PartitionSpec as P

ROW = 8
TOK = 16
PARTS = 4
WIDE = 2
STATE = 128
LANES = 128
HALF = 64

F32 = jnp.float32
BF16 = jnp.bfloat16
MESH = pl.DeviceIdType.MESH


def mm(a, b, ca, cb):
    return lax.dot_general(a, b, (((ca,), (cb,)), ((), ())), preferred_element_type=F32)


def mm_exact(a, b):
    return lax.dot_general(
        a,
        b,
        (((1,), (0,)), ((), ())),
        precision=lax.Precision.HIGHEST,
        preferred_element_type=F32,
    )


def loop(low, high, body):
    def step(i, carry):
        body(i)
        return carry

    lax.fori_loop(low, high, step, 0)


def pairs(count, body, after=None):
    def step(k):
        for i in range(WIDE):
            body(k * WIDE + i)
        if after is not None:
            for i in range(WIDE):
                after(k * WIDE + i)

    loop(0, count // WIDE, step)


def bytes_wait(ref, sem):
    pltpu.make_async_copy(ref, ref, sem).wait()


def kernel(
    sizes,
    x_hbm, z_hbm, og_hbm, b_hbm, c_hbm, dt_hbm, bias_hbm, alog_hbm, skip_hbm,
    inner_hbm, outer_hbm, gdt_hbm, sums_hbm,
    x_ref, z_ref, og_ref, b_ref, c_ref, dt_ref, bias_ref, alog_ref, skip_ref,
    sx, sg, rx, rg, sbc, rzb, scz, rcz, rb, rc, sdt, rdt, ssend, asend, srecv, arecv, skept, rkept, fades, sy, sdx, ry, rdx,
    sdb, sdc, mdb, mdc, tdb, tdc, rdb, rdc, sgd, rgd, szo, rzo, szc, rzc, ssy, rsy, ssr, rsr,
    inner_ref, outer_ref, gdt_ref, sums_ref, slope, turn, cols, ecol, wcol, eg, wx, st_s, st_a, hb, gb, affs, decs, scores,
    y_in, dx_in, dc_in, db_in, ds0, dla0, rho, kap, cterm, skipsum,
    zb_send, zb_recv, zc_send, zc_recv, x_send, x_recv, g_send, g_recv, b_send, b_recv, c_send, c_recv,
    dt_send, dt_recv, s_send, s_recv, a_send, a_recv, k_send, k_recv, y_send, y_recv, dx_send, dx_recv,
    db_send, db_recv, dc_send, dc_recv, mb_send, mb_recv, mc_send, mc_recv, gd_send, gd_recv, zo_send, zo_recv, oc_send, oc_recv,
    sy_send, sy_recv, sr_send, sr_recv, load, done,
):
    slabs, row, zs, heads = sizes
    length = zs * TOK
    per = 2 * row
    seq, z = lax.axis_index("seq"), lax.axis_index("head")
    y, r = lax.div(seq, row), lax.rem(seq, row)
    low = y < slabs // 2
    mine = pl.ds(pl.multiple_of(z * TOK, TOK), TOK)

    def either(early, late):
        pl.when(low)(early)
        pl.when(jnp.logical_not(low))(late)

    def at(row_to, z_to):
        return (y * row + row_to, z_to)

    def other(i):
        return lax.rem(r + lax.div(i, zs), row), lax.rem(z + lax.rem(i, zs), zs)

    def lanes_of(d):
        return pl.ds(pl.multiple_of(d * LANES, LANES), LANES)

    def tokens_of(k):
        return pl.ds(pl.multiple_of(k * TOK, TOK), TOK)

    def send(src, dst, send_sem, recv_sem, device):
        pltpu.make_async_remote_copy(
            src_ref=src,
            dst_ref=dst,
            send_sem=send_sem,
            recv_sem=recv_sem,
            device_id=device,
            device_id_type=MESH,
        ).start()

    def keep(src, dst, recv_sem):
        pltpu.make_async_copy(src, dst, recv_sem).start()

    barrier = pltpu.get_barrier_semaphore()

    def greet(i):
        pl.semaphore_signal(barrier, inc=1, device_id=at(*other(i)), device_id_type=MESH)

    def greet_slab(i):
        there = (lax.rem(y + i, slabs) * row + r, z)
        pl.semaphore_signal(barrier, inc=1, device_id=there, device_id_type=MESH)

    loop(1, row * zs, greet)
    loop(1, slabs, greet_slab)

    loads = [
        pltpu.make_async_copy(there, here, load.at[i])
        for i, (there, here) in enumerate(
            (
                (b_hbm, b_ref),
                (c_hbm, c_ref),
                (dt_hbm, dt_ref),
                (x_hbm, x_ref),
                (z_hbm, z_ref),
                (og_hbm, og_ref),
                (bias_hbm, bias_ref),
                (alog_hbm, alog_ref),
                (skip_hbm, skip_ref),
            )
        )
    ]
    for copy in loads:
        copy.start()

    for copy in loads[:3]:
        copy.wait()
    def pack(one_ref, two_ref):
        for k in range(zs):
            sbc[k, 0] = one_ref[:, k * STATE : (k + 1) * STATE]
            scz[k] = two_ref[:, k * STATE : (k + 1) * STATE]

    either(lambda: pack(b_ref, c_ref), lambda: pack(c_ref, b_ref))
    for k in range(zs):
        sbc[k, 1, :, 0:heads] = dt_ref[...]
    loads[3].wait()
    for d in range(row * zs):
        sx[d] = x_ref[:, d * LANES : (d + 1) * LANES]
    pl.semaphore_wait(barrier, row * zs - 1 + slabs - 1)

    keep(sbc.at[z], rzb.at[:, mine, :], zb_recv)

    def send_zb(i):
        to = lax.rem(z + i, zs)
        send(sbc.at[to], rzb.at[:, mine, :], zb_send, zb_recv, at(r, to))

    loop(1, zs, send_zb)

    def send_x(i):
        r_to, z_to = other(i)
        d = z_to * row + r_to
        send(sx.at[d], rx.at[r, mine, :], x_send, x_recv.at[r], at(r_to, z_to))

    def all_x():
        keep(sx.at[z * row + r], rx.at[r, mine, :], x_recv.at[r])
        loop(1, row * zs, send_x)

    def gate(k):
        for i in range(row):
            d = k * row + i
            zf, of = z_ref[:, lanes_of(d)].astype(F32), og_ref[:, lanes_of(d)].astype(F32)
            s = jax.nn.sigmoid(zf)
            sg[d] = (of * (zf * s)).astype(BF16)
            slope[d] = of * (s * (1.0 + zf * (1.0 - s)))

    def send_g(i):
        r_to, z_to = other(i)
        d = z_to * row + r_to
        send(sg.at[d], rg.at[r, mine, :], g_send, g_recv.at[r], at(r_to, z_to))

    def all_g():
        for copy in loads[4:6]:
            copy.wait()
        loop(0, zs, gate)
        keep(sg.at[z * row + r], rg.at[r, mine, :], g_recv.at[r])
        loop(1, row * zs, send_g)

    either(all_x, all_g)

    keep(scz.at[z], rcz.at[mine, :], zc_recv)

    def send_zc(i):
        to = lax.rem(z + i, zs)
        send(scz.at[to], rcz.at[mine, :], zc_send, zc_recv, at(r, to))

    loop(1, zs, send_zc)

    def share(src, dst, send_sem, recv_sem):
        keep(src, dst.at[r], recv_sem.at[r])

        def one(i):
            to = lax.rem(r + i, row)
            send(src, dst.at[r], send_sem, recv_sem.at[r], at(to, z))

        loop(1, row, one)

    bytes_wait(rzb, zb_recv)
    either(
        lambda: share(rzb.at[0], rb, b_send, b_recv), lambda: share(rzb.at[0], rc, c_send, c_recv)
    )

    for copy in loads[6:]:
        copy.wait()
    turn[...] = jnp.transpose(rzb[1].astype(F32)[:, 0:heads])
    raw = turn[pl.ds(pl.multiple_of(z * per, per), per), :]
    head_at = lax.broadcasted_iota(jnp.int32, (per, length), 0)
    token_at = lax.broadcasted_iota(jnp.int32, (per, length), 1)
    bias = jnp.zeros((per, length), F32)
    rate = jnp.zeros((per, length), F32)
    for h in range(per):
        bias = jnp.where(head_at == h, bias_ref[h], bias)
        rate = jnp.where(head_at == h, alog_ref[h], rate)
    pre = raw + bias
    step = jnp.maximum(pre, 0.0) + jnp.log1p(jnp.exp(-jnp.abs(pre)))
    squash = jax.nn.sigmoid(pre)
    decay = -jnp.exp(rate) * step
    cum = decay
    reach = 1
    while reach < length:
        cum = cum + jnp.where(token_at >= reach, pltpu.roll(cum, reach, 1), 0.0)
        reach *= 2
    for d in range(row):
        pair = slice(2 * d, 2 * d + 2)
        sdt[d] = jnp.concatenate([step[pair], cum[pair], squash[pair], decay[pair]], axis=0)
    keep(sdt.at[r], rdt.at[r], dt_recv.at[r])

    def send_dt(i):
        to = lax.rem(r + i, row)
        send(sdt.at[to], rdt.at[r], dt_send, dt_recv.at[r], at(to, z))

    loop(1, row, send_dt)

    either(all_g, all_x)
    bytes_wait(rcz, zc_recv)
    either(lambda: share(rcz, rc, c_send, c_recv), lambda: share(rcz, rb, b_send, b_recv))

    lane = lax.broadcasted_iota(jnp.int32, (1, LANES), 1)
    first = lane < HALF
    sel = [first.astype(F32), 1.0 - first.astype(F32)]
    skip = jnp.where(first, skip_ref[2 * r], skip_ref[2 * r + 1])
    at_row = lax.broadcasted_iota(jnp.int32, (length, length), 0)
    at_col = lax.broadcasted_iota(jnp.int32, (length, length), 1)
    causal = at_row >= at_col
    before = (at_row < at_col).astype(F32)
    sel_at = lax.broadcasted_iota(jnp.int32, (16, LANES), 0)
    sel_lane = lax.broadcasted_iota(jnp.int32, (16, LANES), 1)
    pick = jnp.where(sel_at == lax.div(sel_lane, HALF), 1.0, 0.0)
    pick16 = pick.astype(BF16)

    def chunk(k):
        return lax.rem(r + row - k, row)

    def last_decay(c):
        return fades[c, 0:1]

    def decays_of(k):
        c = chunk(k)
        rows = rdt[c]
        across = jnp.transpose(rows)
        cols[c] = across
        up = jnp.where(first, across[:, 2:3], across[:, 3:4])
        end = jnp.where(first, rows[2:3, length - 1 :], rows[3:4, length - 1 :])
        size = jnp.where(first, across[:, 0:1], across[:, 1:2])
        ecol[c] = jnp.exp(up)
        wcol[c] = jnp.exp(end - up) * size
        fades[c] = jnp.broadcast_to(jnp.exp(end), (8, LANES))

    loop(0, row, lambda c: bytes_wait(rdt.at[c], dt_recv.at[c]))
    pairs(row, decays_of)
    kept = fades[0]
    for c in range(1, row):
        kept = kept * fades[c]
    skept[...] = kept

    def send_kept(i):
        there = (lax.rem(y + i, slabs) * row + r, z)
        send(skept, rkept.at[y], k_send, k_recv.at[y], there)

    loop(1, slabs, send_kept)

    def states(k):
        c = chunk(k)
        bytes_wait(rx.at[c], x_recv.at[c])
        grown = (wcol[c] * rx[c].astype(F32)).astype(BF16)
        wx[c] = grown
        st_s[c] = mm(rb[c], grown, 0, 0)

    def send_s(i):
        @pl.when(y + i < slabs)
        def _():
            send(ssend, srecv.at[y], s_send, s_recv.at[y], ((y + i) * row + r, z))

    def states_out():
        loop(0, row, lambda c: bytes_wait(rb.at[c], b_recv.at[c]))
        states_late()

    def states_late():
        loop(0, row, states)
        state = jnp.zeros((STATE, LANES), F32)
        for c in range(row):
            state = last_decay(c) * state + st_s[c]
        ssend[...] = state.astype(BF16)
        loop(1, slabs, send_s)

    def cotangents(k):
        c = chunk(k)
        bytes_wait(rg.at[c], g_recv.at[c])
        faded = (ecol[c] * rg[c].astype(F32)).astype(BF16)
        eg[c] = faded
        st_a[c] = mm(rc[c], faded, 0, 0)

    def send_a(i):
        @pl.when(y >= i)
        def _():
            send(asend, arecv.at[y], a_send, a_recv.at[y], ((y - i) * row + r, z))

    def cotangents_out():
        loop(0, row, lambda c: bytes_wait(rc.at[c], c_recv.at[c]))
        cotangents_late()

    def cotangents_late():
        loop(0, row, cotangents)
        back = jnp.zeros((STATE, LANES), F32)
        for c in reversed(range(row)):
            back = last_decay(c) * back + st_a[c]
        asend[...] = back.astype(BF16)
        loop(1, slabs, send_a)

    def inner_y(c):
        xf = rx[c].astype(F32)
        total = skip * xf
        for j in range(2):
            total = total + mm(scores[c, j], (xf * sel[j]).astype(BF16), 1, 0)
        y_in[c] = total

    def inner_x(c):
        gf = rg[c].astype(F32)
        total = skip * gf
        for j in range(2):
            total = total + mm(scores[c, j], (gf * sel[j]).astype(BF16), 0, 0)
        dx_in[c] = total

    def scored(then, k):
        c = chunk(k)
        across = cols[c]
        aff = mm(rc[c], rb[c], 1, 1)
        affs[c] = aff
        for j in range(2):
            fall = across[:, 2 + j : 3 + j] - rdt[c, 2 + j : 3 + j, :]
            e = jnp.where(causal, jnp.exp(fall), 0.0)
            decs[c, j] = e
            scores[c, j] = (e * aff * rdt[c, j : j + 1, :]).astype(BF16)
        then(c)

    def await_kept():
        def one(i):
            source = lax.rem(y + i, slabs)
            bytes_wait(rkept.at[source], k_recv.at[source])

        loop(1, slabs, one)

    def states_in():
        state = jnp.zeros((STATE, LANES), F32)
        for i in reversed(range(1, slabs)):
            source = lax.rem(y + slabs - i, slabs)

            @pl.when(y >= i)
            def _():
                bytes_wait(srecv.at[source], s_recv.at[source])

            fade = rkept[source, 0:1]
            state = jnp.where(y >= i, fade * state + srecv[source].astype(F32), state)
        for c in range(row):
            hb[c] = state.astype(BF16)
            here = st_s[c]
            st_s[c] = state
            state = last_decay(c) * state + here

    def cotangents_in():
        back = jnp.zeros((STATE, LANES), F32)
        for i in reversed(range(1, slabs)):
            source = lax.rem(y + i, slabs)

            @pl.when(y + i < slabs)
            def _():
                bytes_wait(arecv.at[source], a_recv.at[source])

            fade, part = rkept[source, 0:1], arecv[source].astype(F32)
            back = jnp.where(y + i < slabs, fade * back + part, back)
        for c in reversed(range(row)):
            gb[c] = back.astype(BF16)
            here = st_a[c]
            st_a[c] = back
            back = last_decay(c) * back + here

    there = z * row + r

    def leave(buffer, landing, send_sem, recv_sem, k):
        c = lax.rem(r + k, row)

        @pl.when(k == 0)
        def _():
            keep(buffer.at[c, mine, :], landing.at[there], recv_sem)

        @pl.when(k > 0)
        def _():
            send(buffer.at[c, mine, :], landing.at[there], send_sem, recv_sem, at(c, z))

        def one(i):
            to = lax.rem(z + i, zs)
            part = buffer.at[c, tokens_of(to), :]
            send(part, landing.at[there], send_sem, recv_sem, at(c, to))

        loop(1, zs, one)

    leave_y = functools.partial(leave, sy, ry, y_send, y_recv)
    leave_x = functools.partial(leave, sdx, rdx, dx_send, dx_recv)

    half, mate = row // 2, lax.rem(r, 2)
    chip = lax.div(r, 2)

    def to_mate(buffer, landing, send_sem, recv_sem):
        def one(i):
            src = buffer.at[2 * i + 1 - mate]
            send(src, landing.at[i], send_sem, recv_sem.at[i], at(r + 1 - 2 * mate, z))

        loop(0, half, one)

    def to_chips(buffer, landing, recv_sem, summed, final, out_sem, in_sem):
        def one(k):
            i = lax.rem(chip + k, half)
            c = 2 * i + mate
            bytes_wait(landing.at[i], recv_sem.at[i])
            summed[i] = (buffer[c].astype(F32) + landing[i].astype(F32)).astype(BF16)

            @pl.when(k == 0)
            def _():
                keep(summed.at[i], final.at[chip], in_sem.at[chip])

            @pl.when(k > 0)
            def _():
                send(summed.at[i], final.at[chip], out_sem, in_sem.at[chip], at(c, z))

        loop(0, half, one)

    c_to_mate = functools.partial(to_mate, sdc, mdc, mc_send, mc_recv)
    b_to_mate = functools.partial(to_mate, sdb, mdb, mb_send, mb_recv)
    c_to_chips = functools.partial(to_chips, sdc, mdc, mc_recv, tdc, rdc, dc_send, dc_recv)
    b_to_chips = functools.partial(to_chips, sdb, mdb, mb_recv, tdb, rdb, db_send, db_recv)

    def finish_y(k):
        c = lax.rem(r + k, row)
        yi = ecol[c] * mm(rc[c], hb[c], 1, 0)
        sy[c] = (y_in[c] + yi).astype(BF16)
        rho[c] = mm(pick16, (rg[c].astype(F32) * yi).astype(BF16), 1, 1)[0:8]

    def finish_x(k):
        c = lax.rem(r + k, row)
        bi = wcol[c] * mm(rb[c], gb[c], 1, 0)
        sdx[c] = (dx_in[c] + bi).astype(BF16)
        kap[c] = mm(pick16, (rx[c].astype(F32) * bi).astype(BF16), 1, 1)[0:8]

    def finish_c(k):
        c = lax.rem(r + k, row)
        sdc[c] = (dc_in[c] + mm(eg[c], hb[c], 1, 1)).astype(BF16)

    def finish_b(k):
        c = lax.rem(r + k, row)
        sdb[c] = (db_in[c] + mm(wx[c], gb[c], 1, 1)).astype(BF16)

    def pulled(then, k):
        c = lax.rem(r + k, row)
        xs, gs = rx[c], rg[c]
        xf, gf = xs.astype(F32), gs.astype(F32)
        aff = affs[c]
        pulls = jnp.zeros((length, length), F32)
        for j in range(2):
            size = rdt[c, j : j + 1, :]
            k1 = decs[c, j] * mm((gf * sel[j]).astype(BF16), xs, 1, 1)
            k0 = k1 * aff
            ds0[c, j : j + 1, :] = jnp.sum(k0, axis=0, keepdims=True)
            crossing = mm((k0 * size).astype(BF16), before.astype(BF16), 1, 0)
            dla0[c, j : j + 1, :] = jnp.sum(
                jnp.where(causal, crossing, 0.0), axis=0, keepdims=True
            )
            pulls = pulls + k1 * size
        pulls = pulls.astype(BF16)
        dc_in[c] = mm(pulls, rb[c], 1, 0)
        db_in[c] = mm(pulls, rc[c], 0, 0)
        skipsum[pl.ds(c, 1), :] = jnp.sum(xf * gf, axis=0, keepdims=True)
        then(c)

    def added(landing, recv_sem):
        loop(0, half, lambda c: bytes_wait(landing.at[c], recv_sem.at[c]))
        total = landing[0].astype(F32)
        for c in range(1, half):
            total = total + landing[c].astype(F32)
        return total.astype(BF16)

    def send_oc(i):
        to = lax.rem(z + i, zs)
        send(szc.at[tokens_of(to), :], rzc.at[z], oc_send, oc_recv, at(r, to))

    def small_out(landing, recv_sem):
        szc[...] = added(landing, recv_sem)
        keep(szc.at[mine, :], rzc.at[z], oc_recv)
        loop(1, zs, send_oc)

    def both(k, one, two):
        one(k)
        two(k)

    def x_first():
        states_out()
        loop(0, row, lambda c: bytes_wait(rc.at[c], c_recv.at[c]))
        pairs(row, functools.partial(scored, inner_y))
        cotangents_late()
        await_kept()
        states_in()
        pairs(row, finish_y, leave_y)
        pairs(row, functools.partial(pulled, inner_x))
        pairs(row, finish_c)
        c_to_mate()
        cotangents_in()
        c_to_chips()
        pairs(row, lambda k: both(k, finish_x, finish_b))
        b_to_mate()

    def g_first():
        cotangents_out()
        loop(0, row, lambda c: bytes_wait(rb.at[c], b_recv.at[c]))
        pairs(row, functools.partial(scored, inner_x))
        states_late()
        await_kept()
        cotangents_in()
        pairs(row, finish_x, leave_x)
        pairs(row, functools.partial(pulled, inner_y))
        pairs(row, finish_b)
        b_to_mate()
        states_in()
        b_to_chips()
        pairs(row, lambda k: both(k, finish_y, finish_c))
        c_to_mate()

    either(x_first, g_first)
    for c in range(row):
        over = last_decay(c) * jnp.sum(st_s[c] * st_a[c], axis=0, keepdims=True)
        cterm[c] = jnp.broadcast_to(
            jnp.sum(pick[0:8] * over, axis=1, keepdims=True), (8, length)
        )

    flat = (row * 8, length)
    dla = (
        dla0[...].reshape(flat)
        + mm_exact(rho[...].reshape(flat), causal.astype(F32))
        + mm_exact(kap[...].reshape(flat), before)
        + cterm[...].reshape(flat)
    )
    parts = [rdt[c] for c in range(row)]
    steps = jnp.concatenate(parts, axis=0)
    squashes = jnp.concatenate([pltpu.roll(p, 4, 0) for p in parts], axis=0)
    decays = jnp.concatenate([pltpu.roll(p, 2, 0) for p in parts], axis=0)
    which = lax.rem(lax.broadcasted_iota(jnp.int32, flat, 0), 8)
    rates = jnp.exp(jnp.where(which == 0, alog_ref[2 * r], alog_ref[2 * r + 1]))
    dsteps = ds0[...].reshape(flat) + kap[...].reshape(flat) / steps - rates * dla
    draws = jnp.where(which < 2, dsteps * squashes, 0.0)
    dlogs = jnp.where(which < 2, dla * decays, 0.0)
    sgd[...] = draws.reshape(row, 8, length)
    keep(sgd.at[r], rgd.at[r], gd_recv.at[r])

    def send_gd(i):
        to = lax.rem(r + i, row)
        send(sgd.at[to], rgd.at[r], gd_send, gd_recv.at[r], at(to, z))

    loop(1, row, send_gd)

    sum_at = lax.broadcasted_iota(jnp.int32, (8, LANES), 0)
    sum_lane = lax.broadcasted_iota(jnp.int32, (8, LANES), 1)
    sums = jnp.zeros((8, LANES), F32)
    for j in range(2):
        totals = (
            jnp.sum(jnp.where(which == j, draws, 0.0)),
            jnp.sum(jnp.where(which == j, dlogs, 0.0)),
            jnp.sum(skipsum[...] * sel[j]),
        )
        for q in range(3):
            place = (sum_at == q) & (sum_lane == 2 * r + j)
            sums = jnp.where(place, totals[q], sums)
    ssy[...] = sums
    keep(ssy, rsy.at[y], sy_recv)

    def send_sy(i):
        send(ssy, rsy.at[y], sy_send, sy_recv, (lax.rem(y + i, slabs) * row + r, z))

    loop(1, slabs, send_sy)

    def x_out():
        loop(0, row // 2, leave_x)
        b_to_chips()
        loop(row // 2, row, leave_x)
        small_out(rdc, dc_recv)

    def y_out():
        loop(0, row // 2, leave_y)
        c_to_chips()
        loop(row // 2, row, leave_y)
        small_out(rdb, db_recv)

    either(x_out, y_out)

    def late_sum(landing, recv_sem):
        szo[0] = added(landing, recv_sem)

    either(lambda: late_sum(rdb, db_recv), lambda: late_sum(rdc, dc_recv))
    loop(0, row, lambda c: bytes_wait(rgd.at[c], gd_recv.at[c]))
    turn[...] = jnp.zeros_like(turn)
    turn[pl.ds(pl.multiple_of(z * per, per), per), :] = jnp.concatenate(
        [rgd[c][0:2] for c in range(row)], axis=0
    )
    szo[1, :, 0:heads] = jnp.transpose(turn[...]).astype(BF16)
    keep(szo.at[:, mine, :], rzo.at[z], zo_recv)

    def send_zo(i):
        to = lax.rem(z + i, zs)
        send(szo.at[:, tokens_of(to), :], rzo.at[z], zo_send, zo_recv, at(r, to))

    loop(1, zs, send_zo)

    bytes_wait(rsy, sy_recv)
    total = rsy[0]
    for i in range(1, slabs):
        total = total + rsy[i]
    ssr[...] = total
    keep(ssr, rsr.at[r], sr_recv)

    def send_sr(i):
        send(ssr, rsr.at[r], sr_send, sr_recv, at(lax.rem(r + i, row), z))

    loop(1, row, send_sr)

    results = [
        pltpu.make_async_copy(inner_ref.at[0], inner_hbm.at[0], done.at[0]),
        pltpu.make_async_copy(inner_ref.at[1], inner_hbm.at[1], done.at[1]),
        pltpu.make_async_copy(outer_ref, outer_hbm, done.at[2]),
        pltpu.make_async_copy(gdt_ref, gdt_hbm, done.at[3]),
        pltpu.make_async_copy(sums_ref, sums_hbm, done.at[4]),
    ]

    def gate_back(k):
        for i in range(row):
            d = k * row + i
            inner_ref[1, :, lanes_of(d)] = (slope[d] * ry[d].astype(F32)).astype(BF16)

    def take_y():
        bytes_wait(ry, y_recv)
        loop(0, zs, gate_back)
        results[1].start()

    def take_x():
        bytes_wait(rdx, dx_recv)
        for d in range(row * zs):
            inner_ref[0, :, d * LANES : (d + 1) * LANES] = rdx[d]
        results[0].start()

    def take_small(early, late):
        bytes_wait(rzc, oc_recv)
        for k in range(zs):
            outer_ref[early, :, k * STATE : (k + 1) * STATE] = rzc[k]
        bytes_wait(rzo, zo_recv)
        for k in range(zs):
            outer_ref[late, :, k * STATE : (k + 1) * STATE] = rzo[k, 0]

    def x_last():
        take_y()
        take_x()
        take_small(1, 0)

    def y_last():
        take_x()
        take_y()
        take_small(0, 1)

    either(x_last, y_last)
    total = jnp.zeros((TOK, heads), F32)
    for k in range(zs):
        total = total + rzo[k, 1, :, 0:heads].astype(F32)
    gdt_ref[...] = total.astype(BF16)
    results[2].start()
    results[3].start()
    bytes_wait(rsr, sr_recv)
    total = rsr[0]
    for i in range(1, row):
        total = total + rsr[i]
    sums_ref[...] = total
    results[4].start()

    for copy in results:
        copy.wait()
    @pl.when(y < slabs - 1)
    def _():
        loop(0, slabs - 1 - y, lambda i: bytes_wait(ssend, s_send))

    @pl.when(y > 0)
    def _():
        loop(0, y, lambda i: bytes_wait(asend, a_send))

    blocks = sg.at[pl.ds(0, row * zs - 1)]
    for sem in (x_send, g_send, y_send, dx_send):
        bytes_wait(blocks, sem)
    others = pl.ds(0, row - 1)
    bytes_wait(sbc.at[pl.ds(0, zs - 1)], zb_send)
    bytes_wait(scz.at[pl.ds(0, zs - 1)], zc_send)
    bytes_wait(rb.at[others], b_send)
    bytes_wait(rc.at[others], c_send)
    bytes_wait(sdt.at[others], dt_send)
    chips = pl.ds(0, half - 1)
    bytes_wait(rdb.at[chips], db_send)
    bytes_wait(rdc.at[chips], dc_send)
    bytes_wait(mdb, mb_send)
    bytes_wait(mdc, mc_send)
    bytes_wait(sgd.at[others], gd_send)
    bytes_wait(rzo.at[pl.ds(0, zs - 1)], zo_send)
    bytes_wait(rzc.at[pl.ds(0, zs - 1)], oc_send)
    bytes_wait(rsy.at[pl.ds(0, slabs - 1)], sy_send)
    bytes_wait(rsr.at[others], sr_send)
    bytes_wait(rkept.at[pl.ds(0, slabs - 1)], k_send)


def unpack(
    inner_hbm, outer_hbm, dt_hbm, sums_hbm,
    gx_ref, gz_ref, gb_ref, gc_ref, gdt_ref, bias_ref, alog_ref, skip_ref,
    inner, outer, dts, sums, bias, alog, skip, come, go,
):
    width = gx_ref.shape[1] // PARTS
    moves = []
    for q, ref in enumerate((gx_ref, gz_ref)):
        for p in range(PARTS):
            part = pl.ds(p * width, width)
            moves.append((inner_hbm.at[q, :, part], inner.at[q, :, part], ref.at[:, part]))
    moves += [
        (outer_hbm.at[0], outer.at[0], gb_ref),
        (outer_hbm.at[1], outer.at[1], gc_ref),
        (dt_hbm, dts, gdt_ref),
    ]
    came = [pltpu.make_async_copy(a, b, come.at[i]) for i, (a, b, _) in enumerate(moves)]
    gone = [pltpu.make_async_copy(b, c, go.at[i]) for i, (_, b, c) in enumerate(moves)]
    last = len(moves)
    came_sums = pltpu.make_async_copy(sums_hbm, sums, come.at[last])
    came_sums.start()
    for copy in came:
        copy.start()
    came_sums.wait()
    for q, (row, ref) in enumerate(((bias, bias_ref), (alog, alog_ref), (skip, skip_ref))):
        row[...] = sums[q, 0 : row.shape[0]]
        gone.append(pltpu.make_async_copy(row, ref, go.at[last + q]))
        gone[-1].start()
    for first, second in zip(came, gone[:last]):
        first.wait()
        second.start()
    for copy in gone:
        copy.wait()


def shards(row, x_proj, z_gate, out_grad, b_proj, c_proj, dt_raw, dt_bias, a_log, d_skip):
    zs = lax.axis_size("head")
    slabs = lax.axis_size("seq") // row
    heads = 2 * row * zs
    length = zs * TOK
    inner = heads * HALF

    def vmem(*shape, dtype=BF16):
        return pltpu.VMEM(shape, dtype)

    square = (row, length, LANES)
    half = (row // 2, length, LANES)
    states = (row, STATE, LANES)
    per = 2 * row
    scratch = [
        vmem(TOK, inner),
        vmem(TOK, inner),
        vmem(TOK, inner),
        vmem(TOK, zs * STATE),
        vmem(TOK, zs * STATE),
        vmem(TOK, heads),
        pltpu.SMEM((per,), F32),
        pltpu.SMEM((per,), F32),
        pltpu.SMEM((per,), F32),
        vmem(row * zs, TOK, LANES),
        vmem(row * zs, TOK, LANES),
        vmem(*square),
        vmem(*square),
        vmem(zs, 2, TOK, STATE),
        vmem(2, length, STATE),
        vmem(zs, TOK, STATE),
        vmem(length, STATE),
        vmem(*square),
        vmem(*square),
        vmem(row, 8, length, dtype=F32),
        vmem(row, 8, length, dtype=F32),
        vmem(STATE, LANES),
        vmem(STATE, LANES),
        vmem(slabs, STATE, LANES),
        vmem(slabs, STATE, LANES),
        vmem(8, LANES, dtype=F32),
        vmem(slabs, 8, LANES, dtype=F32),
        vmem(row, 8, LANES, dtype=F32),
        vmem(*square),
        vmem(*square),
        vmem(row * zs, TOK, LANES),
        vmem(row * zs, TOK, LANES),
        vmem(*square),
        vmem(*square),
        vmem(*half),
        vmem(*half),
        vmem(*half),
        vmem(*half),
        vmem(*half),
        vmem(*half),
        vmem(row, 8, length, dtype=F32),
        vmem(row, 8, length, dtype=F32),
        vmem(2, length, STATE),
        vmem(zs, 2, TOK, STATE),
        vmem(length, STATE),
        vmem(zs, TOK, STATE),
        vmem(8, LANES, dtype=F32),
        vmem(slabs, 8, LANES, dtype=F32),
        vmem(8, LANES, dtype=F32),
        vmem(row, 8, LANES, dtype=F32),
        vmem(2, TOK, inner),
        vmem(2, TOK, zs * STATE),
        vmem(TOK, heads),
        vmem(8, LANES, dtype=F32),
        vmem(row * zs, TOK, LANES, dtype=F32),
        vmem(heads, length, dtype=F32),
        vmem(row, length, 8, dtype=F32),
        vmem(*square, dtype=F32),
        vmem(*square, dtype=F32),
        vmem(*square),
        vmem(*square),
        vmem(*states, dtype=F32),
        vmem(*states, dtype=F32),
        vmem(*states),
        vmem(*states),
        vmem(row, length, length, dtype=F32),
        vmem(row, 2, length, length, dtype=F32),
        vmem(row, 2, length, length),
        vmem(*square, dtype=F32),
        vmem(*square, dtype=F32),
        vmem(*square, dtype=F32),
        vmem(*square, dtype=F32),
        vmem(row, 8, length, dtype=F32),
        vmem(row, 8, length, dtype=F32),
        vmem(row, 8, length, dtype=F32),
        vmem(row, 8, length, dtype=F32),
        vmem(row, 8, length, dtype=F32),
        vmem(row, LANES, dtype=F32),
    ]
    one, many = pltpu.SemaphoreType.DMA, lambda n: pltpu.SemaphoreType.DMA((n,))
    semaphores = [
        one, one,
        one, one,
        one, many(row),
        one, many(row),
        one, many(row),
        one, many(row),
        one, many(row),
        one, many(slabs),
        one, many(slabs),
        one, many(slabs),
        one, one,
        one, one,
        one, many(row // 2),
        one, many(row // 2),
        one, many(row // 2),
        one, many(row // 2),
        one, many(row),
        one, one,
        one, one,
        one, one,
        one, one,
        many(9),
        many(5),
    ]
    in_hbm = pl.BlockSpec(memory_space=pltpu.HBM)
    like = jax.ShapeDtypeStruct
    results = pl.pallas_call(
        functools.partial(kernel, (slabs, row, zs, heads)),
        out_shape=[
            like((2, TOK, inner), BF16),
            like((2, TOK, zs * STATE), BF16),
            like((TOK, heads), BF16),
            like((8, LANES), F32),
        ],
        in_specs=[in_hbm] * 9,
        out_specs=[in_hbm] * 4,
        scratch_shapes=scratch + semaphores,
        compiler_params=pltpu.CompilerParams(
            collective_id=0, has_side_effects=True, vmem_limit_bytes=62 * 2**20
        ),
        name="scan_backward",
    )(x_proj, z_gate, out_grad, b_proj, c_proj, dt_raw, dt_bias, a_log, d_skip)
    anywhere = pl.BlockSpec(memory_space=pl.ANY)
    return pl.pallas_call(
        unpack,
        out_shape=[
            like((TOK, inner), BF16),
            like((TOK, inner), BF16),
            like((TOK, zs * STATE), BF16),
            like((TOK, zs * STATE), BF16),
            like((TOK, heads), BF16),
            like((per,), F32),
            like((per,), F32),
            like((per,), F32),
        ],
        in_specs=[anywhere] * 4,
        out_specs=[anywhere] * 8,
        scratch_shapes=[
            vmem(2, TOK, inner),
            vmem(2, TOK, zs * STATE),
            vmem(TOK, heads),
            vmem(8, LANES, dtype=F32),
            vmem(per, dtype=F32),
            vmem(per, dtype=F32),
            vmem(per, dtype=F32),
            many(2 * PARTS + 4),
            many(2 * PARTS + 6),
        ],
        compiler_params=pltpu.CompilerParams(vmem_limit_bytes=62 * 2**20),
        name="unpack",
    )(*results)


def solution(mesh, row=ROW):
    tokens = P(("seq", "head"), None)
    return jax.shard_map(
        functools.partial(shards, row),
        mesh=mesh,
        in_specs=(tokens,) * 6 + (P("head"),) * 3,
        out_specs=(tokens,) * 5 + (P("head"),) * 3,
        check_vma=False,
    )
```
